512 devices in a mesh: dom: 64 (over y_lo, z, core), pix: 8 (over x, y_hi).
Axes of the slice: x: 4, y: 8 (y_hi: 2, y_lo: 4; y = y_hi * 4 + y_lo), z: 8, core: 2. Of those that a mesh axis runs over, the one named last changes fastest.
Arguments:
- images: bfloat16 [16384, 16384], P('dom', 'pix'), may hold values from -1500 to 1500
- ctf_group: int32 [16384], P('dom'), may hold values from 0 to 127
- projections: bfloat16 [384, 16384], P('dom', 'pix'), may hold values from -4 to 4
- ctf_table: float32 [128, 16384], P(None, 'pix'), may hold values from 0.1 to 1.5
- noise_power: float32 [16384], P('pix'), may hold values from 1000 to 4000
- prior: float32 [16384], P('pix'), may hold values from 0.01 to 0.1
- log_prior: float32 [16], replicated, may hold values from -3 to 3
- projection_class: int32 [384], replicated, may hold values from 0 to 15, as said below
Outputs:
- class_average: float32 [384, 16384], P('dom', 'pix')
- class_mass: float32 [16], replicated
The draws below stay inside these ranges and needn't reach their ends.
Inputs may be any that keep to these rules, and one draw needn't show every extreme that they name: `projection_class`: each class names exactly 24 rows.
All inputs are finite; a program needn't handle non-finite values.
Results may differ from the reference program's by a relative error of at most 0.005.
Values may be sent and summed in bfloat16 or wider, within the bound.
A program may use at most 64 MiB of HBM per device.

```python
import math
import jax
import jax.numpy as jnp
from jax import lax

PIXELS = 16384
CLASSES = 16
ORIENT = 24
GROUPS = 128
PART_DEV = 256
PROJS = 384
PARTICLES = 16384


def group_ids(key):
    key = jax.random.fold_in(key, 11)
    return jax.random.randint(key, (PARTICLES,), 0, GROUPS).astype(jnp.int32)


def base_projections(key):
    key = jax.random.fold_in(key, 12)
    return jax.random.truncated_normal(key, -4.0, 4.0, (PROJS, PIXELS), jnp.float32)


def amplitude_table(key):
    key = jax.random.fold_in(key, 13)
    phase = jax.random.uniform(key, (GROUPS, PIXELS), jnp.float32, 0.0, 3.14159265)
    return 0.1 + 1.4 * jnp.abs(jnp.sin(phase))


def noise_levels(key):
    key = jax.random.fold_in(key, 14)
    spread = jax.random.uniform(key, (PIXELS,), jnp.float32)
    return 1000.0 * jnp.exp(spread * jnp.log(4.0))


def draw_ctf_group(key, part):
    return group_ids(key)


def draw_projections(key, part):
    return base_projections(key).astype(jnp.bfloat16)


def draw_ctf_table(key, part):
    return amplitude_table(key)


def draw_noise_power(key, part):
    return noise_levels(key)


def draw_projection_class(key, part):
    key = jax.random.fold_in(key, 31)
    order = jax.random.permutation(key, PROJS).astype(jnp.int32)
    return (order // ORIENT).astype(jnp.int32)


def draw_images(key, part):
    groups = group_ids(key)
    proj_rows = base_projections(key)
    amplitude = amplitude_table(key)
    noise = noise_levels(key)
    key = jax.random.fold_in(key, 21)
    key_target = jax.random.fold_in(key, 0)
    key_noise = jax.random.fold_in(key, 2)
    target = jax.random.randint(key_target, (PARTICLES,), 0, PROJS)
    row_amp = jnp.take(amplitude, groups, axis=0)
    signal = row_amp * jnp.take(proj_rows, target, axis=0)
    fuzz = jax.random.truncated_normal(key_noise, -4.0, 4.0, (PARTICLES, PIXELS), jnp.float32)
    image = signal + fuzz * jnp.sqrt(noise)[None, :]
    return image.astype(jnp.bfloat16)


def level_of(stream_key, shape, cuts, low, high):
    gain, own = 1.0, jax.random.fold_in(stream_key, 6)
    for position, parts in cuts:
        draws = jnp.exp(jax.random.uniform(jax.random.fold_in(own, position), (parts,), jnp.float32, low / len(cuts), high / len(cuts)))
        gain = gain * jnp.repeat(draws, shape[position] // parts).reshape([-1 if axis == position else 1 for axis in range(len(shape))])
    return gain


def scatter_about(rng, dims, scale, most, kind=jnp.bfloat16):
    values = scale * jax.random.normal(rng, dims, jnp.float32)
    return jnp.clip(values, min=-most, max=most).astype(kind)


def setup_inputs(seed: int = 0) -> dict:
    key_list = jax.random.split(jax.random.key(seed), 9)
    images = draw_images(jax.random.fold_in(key_list[8], 71), 0)
    ctf_group = draw_ctf_group(jax.random.fold_in(key_list[8], 71), 0)
    projections = draw_projections(jax.random.fold_in(key_list[8], 71), 0)
    ctf_table = draw_ctf_table(jax.random.fold_in(key_list[8], 71), 0)
    noise_power = draw_noise_power(jax.random.fold_in(key_list[8], 71), 0)
    prior = jnp.clip(jnp.exp(math.log(0.1) - 2.3025851 * jax.random.uniform(key_list[5], (PIXELS,), jnp.float32) ** level_of(key_list[5], (PIXELS,), ((0, 8),), -0.2, 0.2)), 0.01, 0.1)
    log_prior = scatter_about(key_list[6], (CLASSES,), 1.0, 3.0, jnp.float32)
    projection_class = draw_projection_class(jax.random.fold_in(key_list[8], 71), 0)
    return {"images": images, "ctf_group": ctf_group, "projections": projections, "ctf_table": ctf_table, "noise_power": noise_power, "prior": prior, "log_prior": log_prior, "projection_class": projection_class}


def posterior(cross_terms, norm_terms, groups, class_bias):
    scores = cross_terms - 0.5 * jnp.take(norm_terms, groups, axis=0) + class_bias[None, :]
    largest = jnp.max(scores, axis=1, keepdims=True)
    raised = jnp.exp(scores - largest)
    return raised / jnp.sum(raised, axis=1, keepdims=True)


def reference(images, ctf_group, projections, ctf_table, noise_power, prior, log_prior, projection_class):
    weight_ctf = ctf_table / noise_power[None, :]
    weight_sq = ctf_table * ctf_table / noise_power[None, :]
    proj_f32 = projections.astype(jnp.float32)
    norm_terms = lax.dot_general(weight_sq, proj_f32 * proj_f32, (((1,), (1,)), ((), ())),
                                 precision=lax.Precision.HIGHEST, preferred_element_type=jnp.float32)
    class_hot = (projection_class[:, None] == jnp.arange(CLASSES, dtype=jnp.int32)[None, :]).astype(jnp.float32)
    class_bias = jnp.sum(class_hot * log_prior[None, :], axis=1)
    image_blocks = images.reshape(PARTICLES // PART_DEV, PART_DEV, PIXELS)
    group_blocks = ctf_group.reshape(PARTICLES // PART_DEV, PART_DEV)

    def visit_block(state_carry, visited):
        weighted_sums, counts, totals = state_carry
        row_block, groups = visited
        weighted = (row_block.astype(jnp.float32) * jnp.take(weight_ctf, groups, axis=0)).astype(jnp.bfloat16)
        cross_terms = lax.dot_general(weighted, projections, (((1,), (1,)), ((), ())),
                                      preferred_element_type=jnp.float32)
        membership = posterior(cross_terms, norm_terms, groups, class_bias)
        member_b = membership.astype(jnp.bfloat16)
        group_hot = (groups[:, None] == jnp.arange(GROUPS, dtype=jnp.int32)[None, :]).astype(jnp.bfloat16)
        weighted_sums = weighted_sums + lax.dot_general(member_b, weighted, (((0,), (0,)), ((), ())),
                                                        preferred_element_type=jnp.float32)
        counts = counts + lax.dot_general(member_b, group_hot, (((0,), (0,)), ((), ())),
                                          preferred_element_type=jnp.float32)
        totals = totals + jnp.sum(membership, axis=0)
        return (weighted_sums, counts, totals), None

    start_carry = (jnp.zeros((PROJS, PIXELS), jnp.float32), jnp.zeros((PROJS, GROUPS), jnp.float32),
                   jnp.zeros((PROJS,), jnp.float32))
    (weighted_sums, counts, totals), _ = lax.scan(visit_block, start_carry, (image_blocks, group_blocks))
    denominator = jnp.dot(counts, weight_sq, precision=lax.Precision.HIGHEST,
                          preferred_element_type=jnp.float32) + prior[None, :]
    class_average = weighted_sums / denominator
    class_mass = jnp.sum(totals[:, None] * class_hot, axis=0) * (CLASSES / PARTICLES)
    return class_average, class_mass
```

```python
import functools

import jax
import jax.numpy as jnp
from jax import lax
from jax.experimental import pallas as pl
from jax.experimental.pallas import tpu as pltpu
from jax.sharding import PartitionSpec as P

MESH = pl.DeviceIdType.MESH
F32 = jnp.float32
BF16 = jnp.bfloat16
NZ, NY, NC, NX, NF = 8, 4, 2, 4, 2


def nt(a, b):
    return lax.dot_general(a, b, (((1,), (1,)), ((), ())), preferred_element_type=F32)


def nn(a, b):
    return lax.dot_general(a, b, (((1,), (0,)), ((), ())), preferred_element_type=F32)


def pieces(a, count):
    terms = []
    for _ in range(count):
        term = a.astype(BF16)
        terms.append(term)
        a = a - term.astype(F32)
    return terms


def iota(shape, axis):
    return lax.broadcasted_iota(jnp.int32, shape, axis)


def kernel(
    images_hbm, group_hbm, proj_hbm, ctf_hbm, noise_hbm, prior_hbm, logp_hbm, class_hbm,
    out_ref, mass_ref,
    images, ctf, noise, prior, logp, pclass, group, own_a, own_b,
    ra1, rb1, ra2, rb2, compact_a, compact_b, table3, square2, weighted, hot_t,
    scores, rx, ry, stats, member, s1a, s1b, r1a, r1b, ta, tb, s2a, s2b, r2a, r2b,
    mass_c, mass_z, mass_y,
    load_sem, send_sem, group_sem, w_sem, a1_sem, b1_sem, a2_sem, b2_sem, x_sem, y_sem, st_sem, m_sem,
    p1a_sem, p1b_sem, p2a_sem, p2b_sem, mc_sem, mz_sem, my_sem,
):
    dom, pix = lax.axis_index("dom"), lax.axis_index("pix")
    core, z, y = dom % NC, (dom // NC) % NZ, dom // (NC * NZ)
    x, far = pix // NF, pix % NF
    rows, half = own_a.shape
    parts = images.shape[0]
    groups, pixels = ctf.shape
    zrows = NZ * rows
    yrows = NY * rows
    krows = NY * NZ * rows
    block = NC * parts // NX

    def at_z(o):
        return ((y * NZ + o) * NC + core, pix)

    def at_y(o):
        return ((o * NZ + z) * NC + core, pix)

    def at_x(o):
        return (dom, o * NF + far)

    other_core = ((y * NZ + z) * NC + (1 - core), pix)
    other_far = (dom, x * NF + (1 - far))
    zs = [(z + d) % NZ for d in range(1, NZ)]
    ys = [(y + d) % NY for d in range(1, NY)]
    xs = [(x + d) % NX for d in range(1, NX)]

    sent = []

    def send(src, dst, recv_sem, device):
        copy = pltpu.make_async_remote_copy(
            src_ref=src,
            dst_ref=dst,
            send_sem=send_sem.at[len(sent)],
            recv_sem=recv_sem,
            device_id=device,
            device_id_type=MESH,
        )
        copy.start()
        sent.append(copy)

    def arrived(dst, recv_sem):
        pltpu.make_async_remote_copy(
            src_ref=dst,
            dst_ref=dst,
            send_sem=recv_sem,
            recv_sem=recv_sem,
            device_id=other_core,
            device_id_type=MESH,
        ).wait_recv()

    loads = [
        pltpu.make_async_copy(src, dst, load_sem.at[i])
        for i, (src, dst) in enumerate((
            (proj_hbm.at[:, pl.ds(0, half)], own_a),
            (proj_hbm.at[:, pl.ds(half, half)], own_b),
            (group_hbm, group.at[core]),
            (ctf_hbm, ctf),
            (noise_hbm, noise),
            (images_hbm, images),
            (prior_hbm, prior),
            (logp_hbm, logp),
            (class_hbm, pclass),
        ))
    ]
    for copy in loads:
        copy.start()

    barrier = pltpu.get_barrier_semaphore()
    peers = [at_z(o) for o in zs] + [at_y(o) for o in ys] + [at_x(o) for o in xs]
    peers += [other_core, other_far]
    for peer in peers:
        pl.semaphore_signal(barrier, inc=1, device_id=peer, device_id_type=MESH)
    for copy in loads[:3]:
        copy.wait()
    pl.semaphore_wait(barrier, len(peers))

    for o in zs:
        send(own_a, ra1.at[z], a1_sem.at[z], at_z(o))
    for o in ys:
        send(own_b, rb1.at[y], b1_sem.at[y], at_y(o))
    send(group.at[core], group.at[core], group_sem, other_core)
    ra1[z] = own_a[...]
    rb1[y] = own_b[...]

    for copy in loads[3:]:
        copy.wait()

    def second_a():
        for o in zs:
            arrived(ra1.at[o], a1_sem.at[o])
        for o in range(NZ):
            compact_a[rows * o : rows * (o + 1), :] = ra1[o].astype(F32)
        ra2[y] = compact_a[...].astype(BF16)
        for o in ys:
            send(ra2.at[y], ra2.at[y], a2_sem.at[y], at_y(o))

    def second_b():
        for o in ys:
            arrived(rb1.at[o], b1_sem.at[o])
        for o in zs:
            send(rb1, rb2.at[z], b2_sem.at[z], at_z(o))
        rb2[z] = rb1[...]

    second_b()
    second_a()

    chunk = min(512, half)
    hot_t[:, pl.ds(pl.multiple_of(core * parts, parts), parts)] = (
        iota((groups, parts), 0) == group[core]
    ).astype(BF16)
    own_hot = jnp.transpose((iota((groups, parts), 0) == group[core]).astype(F32)).astype(BF16)
    hot3 = jnp.concatenate([own_hot] * 3, axis=1)
    mine = pl.ds(pl.multiple_of(core * parts, parts), parts)
    for c in range(0, pixels, chunk):
        columns = slice(c, c + chunk)
        table, variance = ctf[:, columns], noise[:, columns]
        for i, term in enumerate(pieces(table / variance, 3)):
            table3[groups * i : groups * (i + 1), columns] = term
        for i, term in enumerate(pieces(table * table / variance, 2)):
            square2[groups * i : groups * (i + 1), columns] = term
        weights = nn(hot3, table3[:, columns])
        weighted[mine, columns] = (images[:, columns].astype(F32) * weights).astype(BF16)
    send(weighted.at[mine], weighted.at[mine], w_sem, other_core)

    owner = ((iota((krows, 1), 0) // rows) * NC + core) * rows + iota((krows, 1), 0) % rows
    picked = iota((krows, NC * krows), 1) == owner
    row_class = jnp.sum(jnp.where(picked, pclass[...], 0), axis=1, keepdims=True)
    class_hot = row_class == iota((krows, logp.shape[1]), 1)
    bias = jnp.sum(jnp.where(class_hot, logp[...], 0.0), axis=1, keepdims=True)

    arrived(group.at[1 - core], group_sem)
    theirs = pl.ds(pl.multiple_of((1 - core) * parts, parts), parts)
    hot_t[:, theirs] = (iota((groups, parts), 0) == group[1 - core]).astype(BF16)

    for o in ys:
        arrived(ra2.at[o], a2_sem.at[o])
    for o in zs:
        arrived(rb2.at[o], b2_sem.at[o])
    for o in range(NZ):
        for p in range(NY):
            first = p * zrows + o * rows
            compact_b[first : first + rows, :] = rb2[o, p].astype(F32)
    proj_a = ra2[...].reshape(krows, half)
    proj_b = compact_b[...].astype(BF16)

    norm2 = jnp.zeros((krows, 2 * groups), F32)
    for proj, columns in ((proj_a, slice(0, half)), (proj_b, slice(half, pixels))):
        wide = proj.astype(F32)
        for term in pieces(wide * wide, 2):
            norm2 += nt(term, square2[:, columns])
    norm = norm2[:, :groups] + norm2[:, groups:]
    norm3 = jnp.concatenate(pieces(norm, 3), axis=1)
    hot_all = hot_t[...]
    norm_n = nn(norm3, jnp.concatenate([hot_all] * 3, axis=0))

    arrived(weighted.at[theirs], w_sem)
    total = nt(proj_a, weighted[:, :half]) + nt(proj_b, weighted[:, half:]) - 0.5 * norm_n
    for o in range(NX):
        scores[o] = total[:, block * o : block * (o + 1)]
    for o in xs:
        send(scores.at[o], rx.at[x], x_sem.at[x], at_x(o))
    rx[x] = scores[x]
    for o in xs:
        arrived(rx.at[o], x_sem.at[o])
    score = rx[0]
    for o in range(1, NX):
        score += rx[o]
    ry[0] = score
    send(ry.at[0], ry.at[1], y_sem, other_far)
    arrived(ry.at[1], y_sem)
    score = ry[0] + ry[1] + bias

    high = jnp.max(score, axis=0, keepdims=True)
    raised = jnp.exp(score - high)
    part = jnp.sum(raised, axis=0, keepdims=True)
    stats[0, 0:1] = high
    stats[0, 1:2] = part
    send(stats.at[0], stats.at[1], st_sem, other_core)
    arrived(stats.at[1], st_sem)
    high_o, part_o = stats[1, 0:1], stats[1, 1:2]
    top = jnp.maximum(high, high_o)
    scale = jnp.exp(high - top)
    scale = scale / (part * scale + part_o * jnp.exp(high_o - top))
    member[x] = (raised * scale).astype(BF16)
    for o in xs:
        send(member.at[x], member.at[x], m_sem.at[x], at_x(o))
    for o in xs:
        arrived(member.at[o], m_sem.at[o])
    members = jnp.concatenate([member[o] for o in range(NX)], axis=1)

    swapped = iota((krows, krows), 0)
    swapped = ((swapped // rows) % NY) * zrows + (swapped // yrows) * rows + swapped % rows
    swap = (iota((krows, krows), 1) == swapped).astype(BF16)
    members_a = nn(swap, members).astype(BF16)
    sums_a = nn(members_a, weighted[:, :half])
    for o in range(NZ):
        s1a[o, :, :half] = sums_a[yrows * o : yrows * (o + 1)].astype(BF16)
    counts = nt(members_a, hot_all)
    for o in range(NZ):
        s1a[o, :, half:] = counts[yrows * o : yrows * (o + 1)].astype(BF16)
    for o in zs:
        send(s1a.at[o], r1a.at[z], p1a_sem.at[z], at_z(o))
    sums_b = nn(members, weighted[:, half:])
    for o in range(NY):
        s1b[o] = sums_b[zrows * o : zrows * (o + 1)].astype(BF16)
    for o in ys:
        send(s1b.at[o], r1b.at[y], p1b_sem.at[y], at_y(o))

    by_row = jnp.sum(members.astype(F32), axis=1, keepdims=True)
    mass = jnp.sum(jnp.where(class_hot, by_row, 0.0), axis=0, keepdims=True)
    mass_c[0] = jnp.broadcast_to(mass, mass_c.shape[1:])
    send(mass_c.at[0], mass_c.at[1], mc_sem, other_core)
    arrived(mass_c.at[1], mc_sem)
    mass_z[z] = mass_c[0] + mass_c[1]
    for o in zs:
        send(mass_z.at[z], mass_z.at[z], mz_sem.at[z], at_z(o))
    for o in zs:
        arrived(mass_z.at[o], mz_sem.at[o])
    mass = mass_z[0]
    for o in range(1, NZ):
        mass += mass_z[o]
    mass_y[y] = mass
    for o in ys:
        send(mass_y.at[y], mass_y.at[y], my_sem.at[y], at_y(o))

    r1b[y] = s1b[y]
    for o in ys:
        arrived(r1b.at[o], p1b_sem.at[o])
    tb[zrows:, :] = jnp.zeros((tb.shape[0] - zrows, half), F32)
    acc = r1b[0].astype(F32)
    for o in range(1, NY):
        acc += r1b[o].astype(F32)
    tb[:zrows, :] = acc
    for o in range(NZ):
        s2b[o] = tb[rows * o : rows * o + 8, :].astype(BF16)
    for o in zs:
        send(s2b.at[o], r2b.at[z], p2b_sem.at[z], at_z(o))

    r1a[z] = s1a[z]
    for o in zs:
        arrived(r1a.at[o], p1a_sem.at[o])
    ta[yrows:, :] = jnp.zeros((ta.shape[0] - yrows, ta.shape[1]), F32)
    acc = r1a[0].astype(F32)
    for o in range(1, NZ):
        acc += r1a[o].astype(F32)
    ta[:yrows, :] = acc
    for o in range(NY):
        s2a[o] = ta[rows * o : rows * o + 8, :].astype(BF16)
    for o in ys:
        send(s2a.at[o], r2a.at[y], p2a_sem.at[y], at_y(o))

    for o in ys:
        arrived(mass_y.at[o], my_sem.at[o])
    mass = mass_y[0]
    for o in range(1, NY):
        mass += mass_y[o]
    mass_ref[...] = mass[0:1] * (logp.shape[1] / (parts * NZ * NY * NC))

    r2a[y] = s2a[y]
    for o in ys:
        arrived(r2a.at[o], p2a_sem.at[o])
    acc = r2a[0].astype(F32)
    for o in range(1, NY):
        acc += r2a[o].astype(F32)
    denominator = prior[...]
    for term in pieces(acc[:, half:], 3):
        denominator = denominator + nn(jnp.concatenate([term, term], axis=1), square2[...])
    out_ref[:, :half] = (acc[:, :half] / denominator[:, :half])[:rows]
    r2b[z] = s2b[z]
    for o in zs:
        arrived(r2b.at[o], p2b_sem.at[o])
    acc = r2b[0].astype(F32)
    for o in range(1, NZ):
        acc += r2b[o].astype(F32)
    out_ref[:, half:] = (acc / denominator[:, half:])[:rows]

    for copy in sent:
        copy.wait_send()


SENDS = 2 * (5 * (NZ - 1) + 5 * (NY - 1) + 2 * (NX - 1) + 6)


def body(images, ctf_group, projections, ctf_table, noise_power, prior, log_prior, projection_class):
    parts, pixels = images.shape
    groups = ctf_table.shape[0]
    classes = log_prior.shape[0]
    rows = projections.shape[0]
    half = pixels // 2
    krows = NZ * NY * rows
    zrows, yrows = NZ * rows, NY * rows
    chip = NC * parts
    block = chip // NX
    pad = 8

    def up(n):
        return -(-n // pad) * pad

    vmem = pltpu.VMEM
    dma = pltpu.SemaphoreType.DMA
    sums, mass = pl.pallas_call(
        kernel,
        out_shape=(
            jax.ShapeDtypeStruct((rows, pixels), F32),
            jax.ShapeDtypeStruct((1, classes), F32),
        ),
        in_specs=[pl.BlockSpec(memory_space=pl.ANY)] * 8,
        out_specs=[pl.BlockSpec(memory_space=pltpu.VMEM)] * 2,
        scratch_shapes=[
            vmem((parts, pixels), BF16),
            vmem((groups, pixels), F32),
            vmem((1, pixels), F32),
            vmem((1, pixels), F32),
            vmem((1, classes), F32),
            vmem((1, NC * krows), jnp.int32),
            vmem((NC, 1, parts), jnp.int32),
            vmem((rows, half), BF16),
            vmem((rows, half), BF16),
            vmem((NZ, rows, half), BF16),
            vmem((NY, rows, half), BF16),
            vmem((NY, zrows, half), BF16),
            vmem((NZ, NY, rows, half), BF16),
            vmem((zrows, half), F32),
            vmem((krows, half), F32),
            vmem((3 * groups, pixels), BF16),
            vmem((2 * groups, pixels), BF16),
            vmem((chip, pixels), BF16),
            vmem((groups, chip), BF16),
            vmem((NX, krows, block), F32),
            vmem((NX, krows, block), F32),
            vmem((2, krows, block), F32),
            vmem((2, 8, block), F32),
            vmem((NX, krows, block), BF16),
            vmem((NZ, yrows, half + groups), BF16),
            vmem((NY, zrows, half), BF16),
            vmem((NZ, yrows, half + groups), BF16),
            vmem((NY, zrows, half), BF16),
            vmem((up(rows * (NY - 1) + 8), half + groups), F32),
            vmem((up(rows * (NZ - 1) + 8), half), F32),
            vmem((NY, 8, half + groups), BF16),
            vmem((NZ, 8, half), BF16),
            vmem((NY, 8, half + groups), BF16),
            vmem((NZ, 8, half), BF16),
            vmem((2, 8, classes), F32),
            vmem((NZ, 8, classes), F32),
            vmem((NY, 8, classes), F32),
            dma((9,)),
            dma((SENDS,)),
            dma, dma,
            dma((NZ,)), dma((NY,)), dma((NY,)), dma((NZ,)),
            dma((NX,)), dma, dma, dma((NX,)),
            dma((NZ,)), dma((NY,)), dma((NY,)), dma((NZ,)),
            dma, dma((NZ,)), dma((NY,)),
        ],
        compiler_params=pltpu.CompilerParams(
            collective_id=0, has_side_effects=True, vmem_limit_bytes=56 * 1024 * 1024
        ),
        cost_estimate=pl.CostEstimate(
            flops=4 * chip * krows * pixels, bytes_accessed=4 * parts * pixels, transcendentals=krows * block
        ),
    )(
        images,
        ctf_group.reshape(1, parts),
        projections,
        ctf_table,
        noise_power.reshape(1, pixels),
        prior.reshape(1, pixels),
        log_prior.reshape(1, classes),
        projection_class.reshape(1, NC * krows),
    )
    return sums, mass.reshape(classes)


def solution(mesh):
    placed = (
        P("dom", "pix"),
        P("dom"),
        P("dom", "pix"),
        P(None, "pix"),
        P("pix"),
        P("pix"),
        P(),
        P(),
    )
    return jax.shard_map(
        body, mesh=mesh, in_specs=placed, out_specs=(P("dom", "pix"), P()), check_vma=False
    )
```

```python
import functools

import jax
import jax.numpy as jnp
from jax import lax
from jax.experimental import pallas as pl
from jax.experimental.pallas import tpu as pltpu
from jax.sharding import PartitionSpec as P

MESH = pl.DeviceIdType.MESH
F32 = jnp.float32
BF16 = jnp.bfloat16
NZ, NY, NC, NX, NF = 8, 4, 2, 4, 2
GATHER_Z, SUM_Z = 1024, 768
STEPS = 2


def nt(a, b):
    return lax.dot_general(a, b, (((1,), (1,)), ((), ())), preferred_element_type=F32)


def nn(a, b):
    return lax.dot_general(a, b, (((1,), (0,)), ((), ())), preferred_element_type=F32)


def pieces(a, count):
    terms = []
    for _ in range(count):
        term = a.astype(BF16)
        terms.append(term)
        a = a - term.astype(F32)
    return terms


def iota(shape, axis):
    return lax.broadcasted_iota(jnp.int32, shape, axis)


def kernel(
    images_hbm, group_hbm, proj_hbm, ctf_hbm, noise_hbm, prior_hbm, logp_hbm, class_hbm,
    out_ref, mass_ref,
    images, ctf, noise, prior, logp, pclass, group, own_a, own_b,
    ra1, rb1, ra2, rb2, compact_a, compact_b, table3, square2, weighted, hot_t,
    scores, rx, ry, stats, member, s1a, s1b, r1a, r1b, ta, tb, s2a, s2b, r2a, r2b,
    mass_c, mass_z, mass_y,
    load_sem, send_sem, group_sem, w_sem, a1_sem, b1_sem, a2_sem, b2_sem, x_sem, y_sem, st_sem, m_sem,
    p1a_sem, p1b_sem, p2a_sem, p2b_sem, mc_sem, mz_sem, my_sem,
):
    dom, pix = lax.axis_index("dom"), lax.axis_index("pix")
    core, z, y = dom % NC, (dom // NC) % NZ, dom // (NC * NZ)
    x, far = pix // NF, pix % NF
    rows, cut = own_a.shape
    parts = images.shape[0]
    groups, pixels = ctf.shape
    first_z = s1a.shape[2] - groups
    zrows = NZ * rows
    yrows = NY * rows
    krows = NY * NZ * rows
    block = NC * parts // NX

    def at_z(o):
        return ((y * NZ + o) * NC + core, pix)

    def at_y(o):
        return ((o * NZ + z) * NC + core, pix)

    def at_x(o):
        return (dom, o * NF + far)

    other_core = ((y * NZ + z) * NC + (1 - core), pix)
    other_far = (dom, x * NF + (1 - far))
    zs = [(z + d) % NZ for d in (4, 3, 5, 2, 6, 1, 7)[8 - NZ :]]
    ys = [(y + d) % NY for d in (2, 1, 3)[4 - NY :]]
    xs = [(x + d) % NX for d in (2, 1, 3)[4 - NX :]]

    sent = []

    def send(src, dst, recv_sem, device):
        copy = pltpu.make_async_remote_copy(
            src_ref=src,
            dst_ref=dst,
            send_sem=send_sem.at[len(sent)],
            recv_sem=recv_sem,
            device_id=device,
            device_id_type=MESH,
        )
        copy.start()
        sent.append(copy)

    def arrived(dst, recv_sem):
        pltpu.make_async_remote_copy(
            src_ref=dst,
            dst_ref=dst,
            send_sem=recv_sem,
            recv_sem=recv_sem,
            device_id=other_core,
            device_id_type=MESH,
        ).wait_recv()

    loads = [
        pltpu.make_async_copy(src, dst, load_sem.at[i])
        for i, (src, dst) in enumerate((
            (proj_hbm.at[:, pl.ds(0, cut)], own_a),
            (proj_hbm.at[:, pl.ds(cut, pixels - cut)], own_b),
            (group_hbm, group.at[core]),
            (ctf_hbm, ctf),
            (noise_hbm, noise),
            (images_hbm, images),
            (prior_hbm, prior),
            (logp_hbm, logp),
            (class_hbm, pclass),
        ))
    ]
    for copy in loads:
        copy.start()

    barrier = pltpu.get_barrier_semaphore()
    peers = [at_z(o) for o in zs] + [at_y(o) for o in ys] + [at_x(o) for o in xs]
    peers += [other_core, other_far]
    for peer in peers:
        pl.semaphore_signal(barrier, inc=1, device_id=peer, device_id_type=MESH)
    for copy in loads[:3]:
        copy.wait()
    pl.semaphore_wait(barrier, len(peers))

    for o in zs:
        send(own_a, ra1.at[z], a1_sem.at[z], at_z(o))
    for o in ys:
        send(own_b, rb1.at[y], b1_sem.at[y], at_y(o))
    send(group.at[core], group.at[core], group_sem, other_core)
    ra1[z] = own_a[...]
    rb1[y] = own_b[...]

    for copy in loads[3:]:
        copy.wait()

    def second_a():
        for o in zs:
            arrived(ra1.at[o], a1_sem.at[o])
        for o in range(NZ):
            compact_a[rows * o : rows * (o + 1), :] = ra1[o].astype(F32)
        ra2[y] = compact_a[...].astype(BF16)
        for o in ys:
            send(ra2.at[y], ra2.at[y], a2_sem.at[y], at_y(o))

    def second_b():
        for o in ys:
            arrived(rb1.at[o], b1_sem.at[o])
        for o in range(NY):
            compact_b[rows * o : rows * (o + 1), :] = rb1[o].astype(F32)
        rb2[z] = compact_b[:yrows, :].astype(BF16)
        for o in zs:
            send(rb2.at[z], rb2.at[z], b2_sem.at[z], at_z(o))

    second_b()
    second_a()

    chunk = min(512, pixels)
    own_hot = jnp.transpose((iota((groups, parts), 0) == group[core]).astype(F32)).astype(BF16)
    hot3 = jnp.concatenate([own_hot] * 3, axis=1)
    mine = pl.ds(pl.multiple_of(core * parts, parts), parts)
    for c in range(0, pixels, chunk):
        columns = slice(c, c + chunk)
        table, variance = ctf[:, columns], noise[:, columns]
        for i, term in enumerate(pieces(table / variance, 3)):
            table3[groups * i : groups * (i + 1), columns] = term
        for i, term in enumerate(pieces(table * table / variance, 2)):
            square2[groups * i : groups * (i + 1), columns] = term
        weights = nn(hot3, table3[:, columns])
        weighted[mine, columns] = (images[:, columns].astype(F32) * weights).astype(BF16)
    send(weighted.at[mine], weighted.at[mine], w_sem, other_core)
    theirs = pl.ds(pl.multiple_of((1 - core) * parts, parts), parts)

    owner = ((iota((krows, 1), 0) // rows) * NC + core) * rows + iota((krows, 1), 0) % rows
    picked = iota((krows, NC * krows), 1) == owner
    row_class = jnp.sum(jnp.where(picked, pclass[...].reshape(1, NC * krows), 0), axis=1, keepdims=True)
    class_hot = row_class == iota((krows, logp.shape[1]), 1)
    bias = jnp.sum(jnp.where(class_hot, logp[...], 0.0), axis=1, keepdims=True)

    arrived(group.at[1 - core], group_sem)
    for o in range(NX):
        first = o * block % parts
        hot_t[o] = (iota((groups, block), 0) == group[o * block // parts, :, first : first + block]).astype(BF16)

    arrived(weighted.at[theirs], w_sem)

    def squares(proj, columns):
        wide = proj.astype(F32)
        high, low = pieces(wide * wide, 2)
        return nt(high, square2[:, columns]) + nt(low, square2[:, columns])

    for o in ys:
        arrived(ra2.at[o], a2_sem.at[o])
    proj_a = ra2[...].reshape(krows, cut)
    cross = nt(proj_a, weighted[:, :cut])
    for h in range(STEPS):
        some = slice(krows // STEPS * h, krows // STEPS * (h + 1))
        for o in range(NX):
            scores[h, o] = cross[some, block * o : block * (o + 1)]
    norm_a = squares(proj_a, slice(0, cut))

    for o in zs:
        arrived(rb2.at[o], b2_sem.at[o])
    for o in range(NZ):
        wide = rb2[o].astype(F32)
        for p in range(NY):
            first = p * zrows + o * rows
            compact_b[first : first + rows, :] = wide[rows * p : rows * (p + 1)]
    proj_b = compact_b[...].astype(BF16)
    norm2 = norm_a + squares(proj_b, slice(cut, pixels))
    norm = norm2[:, :groups] + norm2[:, groups:]
    norm3 = jnp.concatenate([term for term in pieces(-0.5 * norm, 3)], axis=1)
    part = krows // STEPS
    for h in range(STEPS):
        some = slice(part * h, part * (h + 1))
        for o in [*xs, x]:
            these = pl.ds(pl.multiple_of(o * block, block), block)
            hot3 = jnp.concatenate([hot_t[o]] * 3, axis=0)
            scores[h, o] += nt(proj_b[some], weighted[these, cut:]) + nn(norm3[some], hot3)
            if o is not x:
                send(scores.at[h, o], rx.at[h, x], x_sem.at[h, x], at_x(o))
    for h in range(STEPS):
        for o in xs:
            arrived(rx.at[h, o], x_sem.at[h, o])
        score = scores[h, x]
        for o in xs:
            score += rx[h, o]
        ry[h, 0] = score
        send(ry.at[h, 0], ry.at[h, 1], y_sem.at[h], other_far)
    for h in range(STEPS):
        arrived(ry.at[h, 1], y_sem.at[h])
    score = jnp.concatenate([ry[h, 0] + ry[h, 1] for h in range(STEPS)], axis=0) + bias

    high = jnp.max(score, axis=0, keepdims=True)
    raised = jnp.exp(score - high)
    part = jnp.sum(raised, axis=0, keepdims=True)
    stats[0, 0:1] = high
    stats[0, 1:2] = part
    send(stats.at[0], stats.at[1], st_sem, other_core)
    arrived(stats.at[1], st_sem)
    high_o, part_o = stats[1, 0:1], stats[1, 1:2]
    top = jnp.maximum(high, high_o)
    scale = jnp.exp(high - top)
    scale = scale / (part * scale + part_o * jnp.exp(high_o - top))
    member[x] = (raised * scale).astype(BF16)
    for o in xs:
        send(member.at[x], member.at[x], m_sem.at[x], at_x(o))
    for o in xs:
        arrived(member.at[o], m_sem.at[o])
    members = jnp.concatenate([member[o] for o in range(NX)], axis=1)

    def first_sum_b(h):
        columns = slice(first_z + width * h, first_z + width * (h + 1))
        sums = nn(members, weighted[:, columns])
        for o in range(NY):
            s1b[h, o] = sums[zrows * o : zrows * (o + 1)].astype(BF16)
        for o in ys:
            send(s1b.at[h, o], r1b.at[h, y], p1b_sem.at[h, y], at_y(o))

    width = s1b.shape[3]
    first_sum_b(0)

    swapped = iota((krows, krows), 0)
    swapped = ((swapped // rows) % NY) * zrows + (swapped // yrows) * rows + swapped % rows
    swap = (iota((krows, krows), 1) == swapped).astype(BF16)
    members_z = nn(swap, members).astype(BF16)
    hot_all = jnp.concatenate([hot_t[o] for o in range(NX)], axis=1)
    counts = nt(members_z, hot_all)
    sums = nn(members_z, weighted[:, :first_z])
    for o in range(NZ):
        s1a[o, :, :first_z] = sums[yrows * o : yrows * (o + 1)].astype(BF16)
        s1a[o, :, first_z:] = counts[yrows * o : yrows * (o + 1)].astype(BF16)
    for o in zs:
        send(s1a.at[o], r1a.at[z], p1a_sem.at[z], at_z(o))

    for h in range(1, STEPS):
        first_sum_b(h)

    by_row = jnp.sum(members.astype(F32), axis=1, keepdims=True)
    mass = jnp.sum(jnp.where(class_hot, by_row, 0.0), axis=0, keepdims=True)
    mass_z[z] = jnp.broadcast_to(mass, mass_z.shape[1:])
    for o in zs:
        send(mass_z.at[z], mass_z.at[z], mz_sem.at[z], at_z(o))

    tb[zrows:, :] = jnp.zeros((tb.shape[0] - zrows, tb.shape[1]), F32)
    ta[yrows:, :] = jnp.zeros((ta.shape[0] - yrows, ta.shape[1]), F32)

    def second_sum_b(h):
        for o in ys:
            arrived(r1b.at[h, o], p1b_sem.at[h, o])
        acc = s1b[h, y].astype(F32)
        for o in ys:
            acc += r1b[h, o].astype(F32)
        tb[:zrows, :] = acc
        for o in range(NZ):
            s2b[h, o] = tb[rows * o : rows * o + 8, :].astype(BF16)
        for o in zs:
            send(s2b.at[h, o], r2b.at[h, z], p2b_sem.at[h, z], at_z(o))

    def second_sum_a():
        for o in zs:
            arrived(r1a.at[o], p1a_sem.at[o])
        acc = s1a[z].astype(F32)
        for o in zs:
            acc += r1a[o].astype(F32)
        ta[:yrows, :] = acc
        for o in range(NY):
            s2a[o] = ta[rows * o : rows * o + 8, :].astype(BF16)
        for o in ys:
            send(s2a.at[o], r2a.at[y], p2a_sem.at[y], at_y(o))

    second_sum_b(0)
    second_sum_a()
    for h in range(1, STEPS):
        second_sum_b(h)

    for o in zs:
        arrived(mass_z.at[o], mz_sem.at[o])
    mass = mass_z[0]
    for o in range(1, NZ):
        mass += mass_z[o]
    mass_y[y] = mass
    for o in ys:
        send(mass_y.at[y], mass_y.at[y], my_sem.at[y], at_y(o))

    for o in ys:
        arrived(r2a.at[o], p2a_sem.at[o])
    acc = s2a[y].astype(F32)
    for o in ys:
        acc += r2a[o].astype(F32)
    counted = jnp.concatenate([term.astype(F32) for term in pieces(acc[:, first_z:], 3)], axis=0).astype(BF16)
    filtered = nn(jnp.concatenate([counted, counted], axis=1), square2[...])
    denominator = filtered[0:8] + filtered[8:16] + filtered[16:24] + prior[...]
    out_ref[:, :first_z] = (acc[:, :first_z] / denominator[:, :first_z])[:rows]
    inverse = 1.0 / denominator[:, first_z:]

    for o in ys:
        arrived(mass_y.at[o], my_sem.at[o])
    mass = mass_y[0]
    for o in range(1, NY):
        mass += mass_y[o]
    mass_c[0] = mass
    send(mass_c.at[0], mass_c.at[1], mc_sem, other_core)
    arrived(mass_c.at[1], mc_sem)
    mass_ref[...] = (mass_c[0] + mass_c[1])[0:1] * (logp.shape[1] / (parts * NZ * NY * NC))

    for h in range(STEPS):
        for o in zs:
            arrived(r2b.at[h, o], p2b_sem.at[h, o])
        acc = s2b[h, z].astype(F32)
        for o in zs:
            acc += r2b[h, o].astype(F32)
        columns = slice(width * h, width * (h + 1))
        out_ref[:, first_z + width * h : first_z + width * (h + 1)] = (acc * inverse[:, columns])[:rows]

    for copy in sent:
        copy.wait_send()


SENDS = STEPS * (5 * (NZ - 1) + 5 * (NY - 1) + 2 * (NX - 1) + 6)


def body(images, ctf_group, projections, ctf_table, noise_power, prior, log_prior, projection_class):
    parts, pixels = images.shape
    groups = ctf_table.shape[0]
    classes = log_prior.shape[0]
    rows = projections.shape[0]
    cut, first_z = GATHER_Z, SUM_Z
    width = (pixels - first_z) // STEPS
    krows = NZ * NY * rows
    zrows, yrows = NZ * rows, NY * rows
    chip = NC * parts
    block = chip // NX
    pad = 8

    def up(n):
        return -(-n // pad) * pad

    vmem = pltpu.VMEM
    dma = pltpu.SemaphoreType.DMA
    sums, mass = pl.pallas_call(
        kernel,
        out_shape=(
            jax.ShapeDtypeStruct((rows, pixels), F32),
            jax.ShapeDtypeStruct((1, classes), F32),
        ),
        in_specs=[pl.BlockSpec(memory_space=pl.ANY)] * 8,
        out_specs=[pl.BlockSpec(memory_space=pltpu.VMEM)] * 2,
        scratch_shapes=[
            vmem((parts, pixels), BF16),
            vmem((groups, pixels), F32),
            vmem((1, pixels), F32),
            vmem((1, pixels), F32),
            vmem((1, classes), F32),
            vmem((NC * krows,), jnp.int32),
            vmem((NC, 1, parts), jnp.int32),
            vmem((rows, cut), BF16),
            vmem((rows, pixels - cut), BF16),
            vmem((NZ, rows, cut), BF16),
            vmem((NY, rows, pixels - cut), BF16),
            vmem((NY, zrows, cut), BF16),
            vmem((NZ, yrows, pixels - cut), BF16),
            vmem((zrows, cut), F32),
            vmem((krows, pixels - cut), F32),
            vmem((3 * groups, pixels), BF16),
            vmem((2 * groups, pixels), BF16),
            vmem((chip, pixels), BF16),
            vmem((NX, groups, block), BF16),
            vmem((STEPS, NX, krows // STEPS, block), F32),
            vmem((STEPS, NX, krows // STEPS, block), F32),
            vmem((STEPS, 2, krows // STEPS, block), F32),
            vmem((2, 8, block), F32),
            vmem((NX, krows, block), BF16),
            vmem((NZ, yrows, first_z + groups), BF16),
            vmem((STEPS, NY, zrows, width), BF16),
            vmem((NZ, yrows, first_z + groups), BF16),
            vmem((STEPS, NY, zrows, width), BF16),
            vmem((up(rows * (NY - 1) + 8), first_z + groups), F32),
            vmem((up(rows * (NZ - 1) + 8), width), F32),
            vmem((NY, 8, first_z + groups), BF16),
            vmem((STEPS, NZ, 8, width), BF16),
            vmem((NY, 8, first_z + groups), BF16),
            vmem((STEPS, NZ, 8, width), BF16),
            vmem((2, 8, classes), F32),
            vmem((NZ, 8, classes), F32),
            vmem((NY, 8, classes), F32),
            dma((9,)),
            dma((SENDS,)),
            dma, dma,
            dma((NZ,)), dma((NY,)), dma((NY,)), dma((NZ,)),
            dma((STEPS, NX)), dma((STEPS,)), dma, dma((NX,)),
            dma((NZ,)), dma((STEPS, NY)), dma((NY,)), dma((STEPS, NZ)),
            dma, dma((NZ,)), dma((NY,)),
        ],
        compiler_params=pltpu.CompilerParams(
            collective_id=0, has_side_effects=True, vmem_limit_bytes=56 * 1024 * 1024
        ),
        cost_estimate=pl.CostEstimate(
            flops=4 * chip * krows * pixels, bytes_accessed=4 * parts * pixels, transcendentals=krows * block
        ),
    )(
        images,
        ctf_group.reshape(1, parts),
        projections,
        ctf_table,
        noise_power.reshape(1, pixels),
        prior.reshape(1, pixels),
        log_prior.reshape(1, classes),
        projection_class,
    )
    return sums, mass.reshape(classes)


def solution(mesh):
    placed = (
        P("dom", "pix"),
        P("dom"),
        P("dom", "pix"),
        P(None, "pix"),
        P("pix"),
        P("pix"),
        P(),
        P(),
    )
    return jax.shard_map(
        body, mesh=mesh, in_specs=placed, out_specs=(P("dom", "pix"), P()), check_vma=False
    )
```

```python
import functools

import jax
import jax.numpy as jnp
from jax import lax
from jax.experimental import pallas as pl
from jax.experimental.pallas import tpu as pltpu
from jax.sharding import PartitionSpec as P

MESH = pl.DeviceIdType.MESH
F32 = jnp.float32
BF16 = jnp.bfloat16
NZ, NY, NC, NX, NF = 8, 4, 2, 4, 2
GATHER_Z, SUM_Z = 1024, 768
SCORE_STEPS, SUM_STEPS = 2, 2


def nt(a, b):
    return lax.dot_general(a, b, (((1,), (1,)), ((), ())), preferred_element_type=F32)


def nn(a, b):
    return lax.dot_general(a, b, (((1,), (0,)), ((), ())), preferred_element_type=F32)


def pieces(a, count):
    terms = []
    for _ in range(count):
        term = a.astype(BF16)
        terms.append(term)
        a = a - term.astype(F32)
    return terms


def iota(shape, axis):
    return lax.broadcasted_iota(jnp.int32, shape, axis)


def kernel(
    images_hbm, group_hbm, proj_hbm, ctf_hbm, noise_hbm, prior_hbm, logp_hbm, class_hbm,
    out_ref, mass_ref,
    images, ctf, noise, prior, logp, pclass, group, own_a, own_b,
    ra1, rb1, ra2, rb2, compact_a, compact_b, table3, square2, weighted, hot_t,
    scores, rx, ry, stats, member, s1a, s1b, r1a, r1b, ta, tb, s2a, s2b, r2a, r2b,
    mass_c, mass_z, mass_y,
    load_sem, send_sem, group_sem, w_sem, a1_sem, b1_sem, a2_sem, b2_sem, x_sem, y_sem, st_sem, m_sem,
    p1a_sem, p1b_sem, p2a_sem, p2b_sem, mc_sem, mz_sem, my_sem,
):
    dom, pix = lax.axis_index("dom"), lax.axis_index("pix")
    core, z, y = dom % NC, (dom // NC) % NZ, dom // (NC * NZ)
    x, far = pix // NF, pix % NF
    rows, cut = own_a.shape
    parts = images.shape[0]
    groups, pixels = ctf.shape
    first_z = s1a.shape[2] - groups
    zrows = NZ * rows
    yrows = NY * rows
    krows = NY * NZ * rows
    block = NC * parts // NX

    def at_z(o):
        return ((y * NZ + o) * NC + core, pix)

    def at_y(o):
        return ((o * NZ + z) * NC + core, pix)

    def at_x(o):
        return (dom, o * NF + far)

    other_core = ((y * NZ + z) * NC + (1 - core), pix)
    other_far = (dom, x * NF + (1 - far))
    zs = [(z + d) % NZ for d in (4, 3, 5, 2, 6, 1, 7)[8 - NZ :]]
    ys = [(y + d) % NY for d in (2, 1, 3)[4 - NY :]]
    xs = [(x + d) % NX for d in (2, 1, 3)[4 - NX :]]

    sent = []

    def send(src, dst, recv_sem, device):
        copy = pltpu.make_async_remote_copy(
            src_ref=src,
            dst_ref=dst,
            send_sem=send_sem.at[len(sent)],
            recv_sem=recv_sem,
            device_id=device,
            device_id_type=MESH,
        )
        copy.start()
        sent.append(copy)

    def arrived(dst, recv_sem):
        pltpu.make_async_remote_copy(
            src_ref=dst,
            dst_ref=dst,
            send_sem=recv_sem,
            recv_sem=recv_sem,
            device_id=other_core,
            device_id_type=MESH,
        ).wait_recv()

    loads = [
        pltpu.make_async_copy(src, dst, load_sem.at[i])
        for i, (src, dst) in enumerate((
            (proj_hbm.at[:, pl.ds(0, cut)], own_a),
            (proj_hbm.at[:, pl.ds(cut, pixels - cut)], own_b),
            (group_hbm, group.at[core]),
            (ctf_hbm, ctf),
            (noise_hbm, noise),
            (images_hbm, images),
            (prior_hbm, prior),
            (logp_hbm, logp),
            (class_hbm, pclass),
        ))
    ]
    for copy in loads:
        copy.start()

    barrier = pltpu.get_barrier_semaphore()
    peers = [at_z(o) for o in zs] + [at_y(o) for o in ys] + [at_x(o) for o in xs]
    peers += [other_core, other_far]
    for peer in peers:
        pl.semaphore_signal(barrier, inc=1, device_id=peer, device_id_type=MESH)
    for copy in loads[:3]:
        copy.wait()
    pl.semaphore_wait(barrier, len(peers))

    for o in zs:
        send(own_a, ra1.at[z], a1_sem.at[z], at_z(o))
    for o in ys:
        send(own_b, rb1.at[y], b1_sem.at[y], at_y(o))
    send(group.at[core], group.at[core], group_sem, other_core)
    ra1[z] = own_a[...]
    rb1[y] = own_b[...]

    for copy in loads[3:]:
        copy.wait()

    def second_a():
        for o in zs:
            arrived(ra1.at[o], a1_sem.at[o])
        for o in range(NZ):
            compact_a[rows * o : rows * (o + 1), :] = ra1[o].astype(F32)
        ra2[y] = compact_a[...].astype(BF16)
        for o in ys:
            send(ra2.at[y], ra2.at[y], a2_sem.at[y], at_y(o))

    def second_b():
        for o in ys:
            arrived(rb1.at[o], b1_sem.at[o])
        for o in range(NY):
            compact_b[rows * o : rows * (o + 1), :] = rb1[o].astype(F32)
        rb2[z] = compact_b[:yrows, :].astype(BF16)
        for o in zs:
            send(rb2.at[z], rb2.at[z], b2_sem.at[z], at_z(o))

    second_b()
    second_a()

    chunk = min(512, pixels)
    own_hot = jnp.transpose((iota((groups, parts), 0) == group[core]).astype(F32)).astype(BF16)
    hot3 = jnp.concatenate([own_hot] * 3, axis=1)
    mine = pl.ds(pl.multiple_of(core * parts, parts), parts)
    for c in range(0, pixels, chunk):
        columns = slice(c, c + chunk)
        table, variance = ctf[:, columns], noise[:, columns]
        for i, term in enumerate(pieces(table / variance, 3)):
            table3[groups * i : groups * (i + 1), columns] = term
        for i, term in enumerate(pieces(table * table / variance, 2)):
            square2[groups * i : groups * (i + 1), columns] = term
        weights = nn(hot3, table3[:, columns])
        weighted[mine, columns] = (images[:, columns].astype(F32) * weights).astype(BF16)
    send(weighted.at[mine], weighted.at[mine], w_sem, other_core)
    theirs = pl.ds(pl.multiple_of((1 - core) * parts, parts), parts)

    owner = ((iota((krows, 1), 0) // rows) * NC + core) * rows + iota((krows, 1), 0) % rows
    picked = iota((krows, NC * krows), 1) == owner
    row_class = jnp.sum(jnp.where(picked, pclass[...].reshape(1, NC * krows), 0), axis=1, keepdims=True)
    class_hot = row_class == iota((krows, logp.shape[1]), 1)
    bias = jnp.sum(jnp.where(class_hot, logp[...], 0.0), axis=1, keepdims=True)

    arrived(group.at[1 - core], group_sem)
    for o in range(NX):
        first = o * block % parts
        hot_t[o] = (iota((groups, block), 0) == group[o * block // parts, :, first : first + block]).astype(BF16)

    arrived(weighted.at[theirs], w_sem)

    def squares(proj, columns):
        wide = proj.astype(F32)
        high, low = pieces(wide * wide, 2)
        return nt(high, square2[:, columns]) + nt(low, square2[:, columns])

    for o in ys:
        arrived(ra2.at[o], a2_sem.at[o])
    proj_a = ra2[...].reshape(krows, cut)
    cross = nt(proj_a, weighted[:, :cut])
    for h in range(SCORE_STEPS):
        some = slice(krows // SCORE_STEPS * h, krows // SCORE_STEPS * (h + 1))
        for o in range(NX):
            scores[h, o] = cross[some, block * o : block * (o + 1)]
    norm_a = squares(proj_a, slice(0, cut))

    for o in zs:
        arrived(rb2.at[o], b2_sem.at[o])
    for o in range(NZ):
        wide = rb2[o].astype(F32)
        for p in range(NY):
            first = p * zrows + o * rows
            compact_b[first : first + rows, :] = wide[rows * p : rows * (p + 1)]
    proj_b = compact_b[...].astype(BF16)
    norm2 = norm_a + squares(proj_b, slice(cut, pixels))
    norm = norm2[:, :groups] + norm2[:, groups:]
    norm3 = jnp.concatenate([term for term in pieces(-0.5 * norm, 3)], axis=1)
    part = krows // SCORE_STEPS
    for h in range(SCORE_STEPS):
        some = slice(part * h, part * (h + 1))
        for o in [*xs, x]:
            these = pl.ds(pl.multiple_of(o * block, block), block)
            hot3 = jnp.concatenate([hot_t[o]] * 3, axis=0)
            scores[h, o] += nt(proj_b[some], weighted[these, cut:]) + nn(norm3[some], hot3)
            if o is not x:
                send(scores.at[h, o], rx.at[h, x], x_sem.at[h, x], at_x(o))
    for h in range(SCORE_STEPS):
        for o in xs:
            arrived(rx.at[h, o], x_sem.at[h, o])
        score = scores[h, x]
        for o in xs:
            score += rx[h, o]
        ry[h, 0] = score
        send(ry.at[h, 0], ry.at[h, 1], y_sem.at[h], other_far)
    for h in range(SCORE_STEPS):
        arrived(ry.at[h, 1], y_sem.at[h])
    score = jnp.concatenate([ry[h, 0] + ry[h, 1] for h in range(SCORE_STEPS)], axis=0) + bias

    high = jnp.max(score, axis=0, keepdims=True)
    raised = jnp.exp(score - high)
    part = jnp.sum(raised, axis=0, keepdims=True)
    stats[0, 0:1] = high
    stats[0, 1:2] = part
    send(stats.at[0], stats.at[1], st_sem, other_core)
    arrived(stats.at[1], st_sem)
    high_o, part_o = stats[1, 0:1], stats[1, 1:2]
    top = jnp.maximum(high, high_o)
    scale = jnp.exp(high - top)
    scale = scale / (part * scale + part_o * jnp.exp(high_o - top))
    member[x] = (raised * scale).astype(BF16)
    for o in xs:
        send(member.at[x], member.at[x], m_sem.at[x], at_x(o))
    for o in xs:
        arrived(member.at[o], m_sem.at[o])
    members = jnp.concatenate([member[o] for o in range(NX)], axis=1)

    def first_sum_b(h):
        columns = slice(first_z + width * h, first_z + width * (h + 1))
        sums = nn(members, weighted[:, columns])
        for o in range(NY):
            s1b[h, o] = sums[zrows * o : zrows * (o + 1)].astype(BF16)
        for o in ys:
            send(s1b.at[h, o], r1b.at[h, y], p1b_sem.at[h, y], at_y(o))

    width = s1b.shape[3]
    first_sum_b(0)

    swapped = iota((krows, krows), 0)
    swapped = ((swapped // rows) % NY) * zrows + (swapped // yrows) * rows + swapped % rows
    swap = (iota((krows, krows), 1) == swapped).astype(BF16)
    members_z = nn(swap, members).astype(BF16)
    hot_all = jnp.concatenate([hot_t[o] for o in range(NX)], axis=1)
    counts = nt(members_z, hot_all)
    sums = nn(members_z, weighted[:, :first_z])
    for o in range(NZ):
        s1a[o, :, :first_z] = sums[yrows * o : yrows * (o + 1)].astype(BF16)
        s1a[o, :, first_z:] = counts[yrows * o : yrows * (o + 1)].astype(BF16)
    for o in zs:
        send(s1a.at[o], r1a.at[z], p1a_sem.at[z], at_z(o))

    for h in range(1, SUM_STEPS):
        first_sum_b(h)

    by_row = jnp.sum(members.astype(F32), axis=1, keepdims=True)
    mass = jnp.sum(jnp.where(class_hot, by_row, 0.0), axis=0, keepdims=True)
    mass_z[z] = jnp.broadcast_to(mass, mass_z.shape[1:])
    for o in zs:
        send(mass_z.at[z], mass_z.at[z], mz_sem.at[z], at_z(o))

    tb[zrows:, :] = jnp.zeros((tb.shape[0] - zrows, tb.shape[1]), F32)
    ta[yrows:, :] = jnp.zeros((ta.shape[0] - yrows, ta.shape[1]), F32)

    def second_sum_b(h):
        for o in ys:
            arrived(r1b.at[h, o], p1b_sem.at[h, o])
        acc = s1b[h, y].astype(F32)
        for o in ys:
            acc += r1b[h, o].astype(F32)
        tb[:zrows, :] = acc
        for o in range(NZ):
            s2b[h, o] = tb[rows * o : rows * (o + 1), :].astype(BF16)
        for o in zs:
            send(s2b.at[h, o], r2b.at[h, z], p2b_sem.at[h, z], at_z(o))

    def second_sum_a():
        for o in zs:
            arrived(r1a.at[o], p1a_sem.at[o])
        acc = s1a[z].astype(F32)
        for o in zs:
            acc += r1a[o].astype(F32)
        ta[:yrows, :] = acc
        for o in range(NY):
            s2a[o] = ta[rows * o : rows * o + 8, :].astype(BF16)
        for o in ys:
            send(s2a.at[o], r2a.at[y], p2a_sem.at[y], at_y(o))

    second_sum_b(0)
    second_sum_a()
    for h in range(1, SUM_STEPS):
        second_sum_b(h)

    for o in zs:
        arrived(mass_z.at[o], mz_sem.at[o])
    mass = mass_z[0]
    for o in range(1, NZ):
        mass += mass_z[o]
    mass_y[y] = mass
    for o in ys:
        send(mass_y.at[y], mass_y.at[y], my_sem.at[y], at_y(o))

    for o in ys:
        arrived(r2a.at[o], p2a_sem.at[o])
    acc = s2a[y].astype(F32)
    for o in ys:
        acc += r2a[o].astype(F32)
    counted = jnp.concatenate([term.astype(F32) for term in pieces(acc[:, first_z:], 3)], axis=0).astype(BF16)
    filtered = nn(jnp.concatenate([counted, counted], axis=1), square2[...])
    denominator = filtered[0:8] + filtered[8:16] + filtered[16:24] + prior[...]
    out_ref[:, :first_z] = (acc[:, :first_z] / denominator[:, :first_z])[:rows]
    inverse = 1.0 / denominator[:, first_z:]

    for o in ys:
        arrived(mass_y.at[o], my_sem.at[o])
    mass = mass_y[0]
    for o in range(1, NY):
        mass += mass_y[o]
    mass_c[0] = mass
    send(mass_c.at[0], mass_c.at[1], mc_sem, other_core)
    arrived(mass_c.at[1], mc_sem)
    mass = (mass_c[0] + mass_c[1])[0] * (logp.shape[1] / (parts * NZ * NY * NC))
    mass_ref[...] = mass

    for h in range(SUM_STEPS):
        for o in zs:
            arrived(r2b.at[h, o], p2b_sem.at[h, o])
        acc = s2b[h, z].astype(F32)
        for o in zs:
            acc += r2b[h, o].astype(F32)
        columns = slice(width * h, width * (h + 1))
        out_ref[:, first_z + width * h : first_z + width * (h + 1)] = acc * inverse[:rows, columns]

    for copy in sent:
        copy.wait_send()


SENDS = max(SCORE_STEPS, SUM_STEPS) * (5 * (NZ - 1) + 5 * (NY - 1) + 2 * (NX - 1) + 6)


def body(images, ctf_group, projections, ctf_table, noise_power, prior, log_prior, projection_class):
    parts, pixels = images.shape
    groups = ctf_table.shape[0]
    classes = log_prior.shape[0]
    rows = projections.shape[0]
    cut, first_z = GATHER_Z, SUM_Z
    width = (pixels - first_z) // SUM_STEPS
    krows = NZ * NY * rows
    zrows, yrows = NZ * rows, NY * rows
    chip = NC * parts
    block = chip // NX
    pad = 8

    def up(n):
        return -(-n // pad) * pad

    vmem = pltpu.VMEM
    dma = pltpu.SemaphoreType.DMA
    sums, mass = pl.pallas_call(
        kernel,
        out_shape=(
            jax.ShapeDtypeStruct((rows, pixels), F32),
            jax.ShapeDtypeStruct((classes,), F32),
        ),
        in_specs=[pl.BlockSpec(memory_space=pl.ANY)] * 8,
        out_specs=[pl.BlockSpec(memory_space=pltpu.VMEM)] * 2,
        scratch_shapes=[
            vmem((parts, pixels), BF16),
            vmem((groups, pixels), F32),
            vmem((1, pixels), F32),
            vmem((1, pixels), F32),
            vmem((1, classes), F32),
            vmem((NC * krows,), jnp.int32),
            vmem((NC, 1, parts), jnp.int32),
            vmem((rows, cut), BF16),
            vmem((rows, pixels - cut), BF16),
            vmem((NZ, rows, cut), BF16),
            vmem((NY, rows, pixels - cut), BF16),
            vmem((NY, zrows, cut), BF16),
            vmem((NZ, yrows, pixels - cut), BF16),
            vmem((zrows, cut), F32),
            vmem((krows, pixels - cut), F32),
            vmem((3 * groups, pixels), BF16),
            vmem((2 * groups, pixels), BF16),
            vmem((chip, pixels), BF16),
            vmem((NX, groups, block), BF16),
            vmem((SCORE_STEPS, NX, krows // SCORE_STEPS, block), F32),
            vmem((SCORE_STEPS, NX, krows // SCORE_STEPS, block), F32),
            vmem((SCORE_STEPS, 2, krows // SCORE_STEPS, block), F32),
            vmem((2, 8, block), F32),
            vmem((NX, krows, block), BF16),
            vmem((NZ, yrows, first_z + groups), BF16),
            vmem((SUM_STEPS, NY, zrows, width), BF16),
            vmem((NZ, yrows, first_z + groups), BF16),
            vmem((SUM_STEPS, NY, zrows, width), BF16),
            vmem((up(rows * (NY - 1) + 8), first_z + groups), F32),
            vmem((up(rows * (NZ - 1) + 8), width), F32),
            vmem((NY, 8, first_z + groups), BF16),
            vmem((SUM_STEPS, NZ, rows, width), BF16),
            vmem((NY, 8, first_z + groups), BF16),
            vmem((SUM_STEPS, NZ, rows, width), BF16),
            vmem((2, 8, classes), F32),
            vmem((NZ, 8, classes), F32),
            vmem((NY, 8, classes), F32),
            dma((9,)),
            dma((SENDS,)),
            dma, dma,
            dma((NZ,)), dma((NY,)), dma((NY,)), dma((NZ,)),
            dma((SCORE_STEPS, NX)), dma((SCORE_STEPS,)), dma, dma((NX,)),
            dma((NZ,)), dma((SUM_STEPS, NY)), dma((NY,)), dma((SUM_STEPS, NZ)),
            dma, dma((NZ,)), dma((NY,)),
        ],
        compiler_params=pltpu.CompilerParams(
            collective_id=0, has_side_effects=True, vmem_limit_bytes=56 * 1024 * 1024
        ),
        cost_estimate=pl.CostEstimate(
            flops=4 * chip * krows * pixels, bytes_accessed=4 * parts * pixels, transcendentals=krows * block
        ),
    )(
        images,
        ctf_group.reshape(1, parts),
        projections,
        ctf_table,
        noise_power.reshape(1, pixels),
        prior.reshape(1, pixels),
        log_prior.reshape(1, classes),
        projection_class,
    )
    return sums, mass


def solution(mesh):
    placed = (
        P("dom", "pix"),
        P("dom"),
        P("dom", "pix"),
        P(None, "pix"),
        P("pix"),
        P("pix"),
        P(),
        P(),
    )
    return jax.shard_map(
        body, mesh=mesh, in_specs=placed, out_specs=(P("dom", "pix"), P()), check_vma=False
    )
```

```python
import functools

import jax
import jax.numpy as jnp
from jax import lax
from jax.experimental import pallas as pl
from jax.experimental.pallas import tpu as pltpu
from jax.sharding import PartitionSpec as P

MESH = pl.DeviceIdType.MESH
F32 = jnp.float32
BF16 = jnp.bfloat16
NZ, NY, NC, NX, NF = 8, 4, 2, 4, 2
GATHER_Z, SUM_Z = 1024, 768
SCORE_STEPS, SUM_STEPS = 2, 2


def nt(a, b):
    return lax.dot_general(a, b, (((1,), (1,)), ((), ())), preferred_element_type=F32)


def nn(a, b):
    return lax.dot_general(a, b, (((1,), (0,)), ((), ())), preferred_element_type=F32)


def pieces(a, count):
    terms = []
    for _ in range(count):
        term = a.astype(BF16)
        terms.append(term)
        a = a - term.astype(F32)
    return terms


def iota(shape, axis):
    return lax.broadcasted_iota(jnp.int32, shape, axis)


def kernel(
    images_hbm, group_hbm, proj_hbm, ctf_hbm, noise_hbm, prior_hbm, logp_hbm, class_hbm,
    out_ref, mass_ref,
    images, ctf, noise, prior, logp, pclass, group, own_a, own_b,
    ra1, rb1, ra2, rb2, compact_a, compact_b, table3, square2, weighted, hot_t,
    scores, rx, ry, stats, member, s1a, s1b, r1a, r1b, ta, tb, s2a, s2b, r2a, r2b,
    mass_c, mass_z, mass_y,
    load_sem, send_sem, group_sem, w_sem, a1_sem, b1_sem, a2_sem, b2_sem, x_sem, y_sem, st_sem, m_sem,
    p1a_sem, p1b_sem, p2a_sem, p2b_sem, mc_sem, mz_sem, my_sem,
):
    dom, pix = lax.axis_index("dom"), lax.axis_index("pix")
    core, z, y = dom % NC, (dom // NC) % NZ, dom // (NC * NZ)
    x, far = pix // NF, pix % NF
    rows, cut = own_a.shape
    parts = images.shape[0]
    groups, pixels = ctf.shape
    first_z = s1a.shape[2] - groups
    zrows = NZ * rows
    yrows = NY * rows
    krows = NY * NZ * rows
    block = NC * parts // NX

    def at_z(o):
        return ((y * NZ + o) * NC + core, pix)

    def at_y(o):
        return ((o * NZ + z) * NC + core, pix)

    def at_x(o):
        return (dom, o * NF + far)

    def at_x_other(o):
        return ((y * NZ + z) * NC + (1 - core), o * NF + far)

    other_core = ((y * NZ + z) * NC + (1 - core), pix)
    other_far = (dom, x * NF + (1 - far))
    zs = [(z + d) % NZ for d in (4, 3, 5, 2, 6, 1, 7)[8 - NZ :]]
    ys = [(y + d) % NY for d in (2, 1, 3)[4 - NY :]]
    xs = [(x + d) % NX for d in (2, 1, 3)[4 - NX :]]

    sent = []

    def send(src, dst, recv_sem, device):
        copy = pltpu.make_async_remote_copy(
            src_ref=src,
            dst_ref=dst,
            send_sem=send_sem.at[len(sent)],
            recv_sem=recv_sem,
            device_id=device,
            device_id_type=MESH,
        )
        copy.start()
        sent.append(copy)

    def arrived(dst, recv_sem):
        pltpu.make_async_remote_copy(
            src_ref=dst,
            dst_ref=dst,
            send_sem=recv_sem,
            recv_sem=recv_sem,
            device_id=other_core,
            device_id_type=MESH,
        ).wait_recv()

    loads = [
        pltpu.make_async_copy(src, dst, load_sem.at[i])
        for i, (src, dst) in enumerate((
            (proj_hbm.at[:, pl.ds(0, cut)], own_a),
            (proj_hbm.at[:, pl.ds(cut, pixels - cut)], own_b),
            (group_hbm, group.at[core]),
            (ctf_hbm, ctf),
            (noise_hbm, noise),
            (images_hbm, images),
            (prior_hbm, prior),
            (logp_hbm, logp),
            (class_hbm, pclass),
        ))
    ]
    for copy in loads:
        copy.start()

    barrier = pltpu.get_barrier_semaphore()
    peers = [at_z(o) for o in zs] + [at_y(o) for o in ys] + [at_x(o) for o in xs]
    peers += [at_x_other(o) for o in xs] + [other_core, other_far]
    for peer in peers:
        pl.semaphore_signal(barrier, inc=1, device_id=peer, device_id_type=MESH)
    for copy in loads[:3]:
        copy.wait()
    pl.semaphore_wait(barrier, len(peers))

    for o in zs:
        send(own_a, ra1.at[z], a1_sem.at[z], at_z(o))
    for o in ys:
        send(own_b, rb1.at[y], b1_sem.at[y], at_y(o))
    send(group.at[core], group.at[core], group_sem, other_core)
    ra1[z] = own_a[...]
    rb1[y] = own_b[...]

    for copy in loads[3:]:
        copy.wait()

    def second_a():
        for o in zs:
            arrived(ra1.at[o], a1_sem.at[o])
        for o in range(NZ):
            compact_a[rows * o : rows * (o + 1), :] = ra1[o].astype(F32)
        ra2[y] = compact_a[...].astype(BF16)
        for o in ys:
            send(ra2.at[y], ra2.at[y], a2_sem.at[y], at_y(o))

    def second_b():
        for o in ys:
            arrived(rb1.at[o], b1_sem.at[o])
        for o in range(NY):
            compact_b[rows * o : rows * (o + 1), :] = rb1[o].astype(F32)
        rb2[z] = compact_b[:yrows, :].astype(BF16)
        for o in zs:
            send(rb2.at[z], rb2.at[z], b2_sem.at[z], at_z(o))

    second_b()
    second_a()

    chunk = min(512, pixels)
    own_hot = jnp.transpose((iota((groups, parts), 0) == group[core]).astype(F32)).astype(BF16)
    hot3 = jnp.concatenate([own_hot] * 3, axis=1)
    mine = pl.ds(pl.multiple_of(core * parts, parts), parts)
    for c in range(0, pixels, chunk):
        columns = slice(c, c + chunk)
        table, variance = ctf[:, columns], noise[:, columns]
        for i, term in enumerate(pieces(table / variance, 3)):
            table3[groups * i : groups * (i + 1), columns] = term
        for i, term in enumerate(pieces(table * table / variance, 2)):
            square2[groups * i : groups * (i + 1), columns] = term
        weights = nn(hot3, table3[:, columns])
        weighted[mine, columns] = (images[:, columns].astype(F32) * weights).astype(BF16)
    send(weighted.at[mine], weighted.at[mine], w_sem, other_core)
    theirs = pl.ds(pl.multiple_of((1 - core) * parts, parts), parts)

    owner = ((iota((krows, 1), 0) // rows) * NC + core) * rows + iota((krows, 1), 0) % rows
    picked = iota((krows, NC * krows), 1) == owner
    row_class = jnp.sum(jnp.where(picked, pclass[...].reshape(1, NC * krows), 0), axis=1, keepdims=True)
    class_hot = row_class == iota((krows, logp.shape[1]), 1)
    bias = jnp.sum(jnp.where(class_hot, logp[...], 0.0), axis=1, keepdims=True)

    arrived(group.at[1 - core], group_sem)
    for o in range(NX):
        first = o * block % parts
        hot_t[o] = (iota((groups, block), 0) == group[o * block // parts, :, first : first + block]).astype(BF16)

    arrived(weighted.at[theirs], w_sem)

    def squares(proj, columns):
        wide = proj.astype(F32)
        high, low = pieces(wide * wide, 2)
        return nt(high, square2[:, columns]) + nt(low, square2[:, columns])

    for o in ys:
        arrived(ra2.at[o], a2_sem.at[o])
    proj_a = ra2[...].reshape(krows, cut)
    cross = nt(proj_a, weighted[:, :cut])
    for h in range(SCORE_STEPS):
        some = slice(krows // SCORE_STEPS * h, krows // SCORE_STEPS * (h + 1))
        for o in range(NX):
            scores[h, o] = cross[some, block * o : block * (o + 1)]
    norm_a = squares(proj_a, slice(0, cut))

    for o in zs:
        arrived(rb2.at[o], b2_sem.at[o])
    for o in range(NZ):
        wide = rb2[o].astype(F32)
        for p in range(NY):
            first = p * zrows + o * rows
            compact_b[first : first + rows, :] = wide[rows * p : rows * (p + 1)]
    proj_b = compact_b[...].astype(BF16)
    norm2 = norm_a + squares(proj_b, slice(cut, pixels))
    norm = norm2[:, :groups] + norm2[:, groups:]
    norm3 = jnp.concatenate([term for term in pieces(-0.5 * norm, 3)], axis=1)
    part = krows // SCORE_STEPS
    for h in range(SCORE_STEPS):
        some = slice(part * h, part * (h + 1))
        for o in [*xs, x]:
            these = pl.ds(pl.multiple_of(o * block, block), block)
            hot3 = jnp.concatenate([hot_t[o]] * 3, axis=0)
            scores[h, o] += nt(proj_b[some], weighted[these, cut:]) + nn(norm3[some], hot3)
            if o is not x:
                send(scores.at[h, o], rx.at[h, x], x_sem.at[h, x], at_x(o))
    for h in range(SCORE_STEPS):
        for o in xs:
            arrived(rx.at[h, o], x_sem.at[h, o])
        score = scores[h, x]
        for o in xs:
            score += rx[h, o]
        ry[h, 0] = score
        send(ry.at[h, 0], ry.at[h, 1], y_sem.at[h], other_far)
    for h in range(SCORE_STEPS):
        arrived(ry.at[h, 1], y_sem.at[h])
    score = jnp.concatenate([ry[h, 0] + ry[h, 1] for h in range(SCORE_STEPS)], axis=0) + bias

    high = jnp.max(score, axis=0, keepdims=True)
    raised = jnp.exp(score - high)
    part = jnp.sum(raised, axis=0, keepdims=True)
    stats[x, core, 0:1] = high
    stats[x, core, 1:2] = part
    mine_st = stats.at[x, core]
    send(mine_st, mine_st, st_sem.at[x, core], other_core)
    for o in xs:
        send(mine_st, mine_st, st_sem.at[x, core], at_x(o))
        send(mine_st, mine_st, st_sem.at[x, core], at_x_other(o))
    member[x] = raised.astype(BF16)
    for o in xs:
        send(member.at[x], member.at[x], m_sem.at[x], at_x(o))
    arrived(stats.at[x, 1 - core], st_sem.at[x, 1 - core])
    for o in xs:
        arrived(stats.at[o, core], st_sem.at[o, core])
        arrived(stats.at[o, 1 - core], st_sem.at[o, 1 - core])
        arrived(member.at[o], m_sem.at[o])
    scaled = []
    for o in range(NX):
        high, part = stats[o, core, 0:1], stats[o, core, 1:2]
        high_o, part_o = stats[o, 1 - core, 0:1], stats[o, 1 - core, 1:2]
        top = jnp.maximum(high, high_o)
        scale = jnp.exp(high - top)
        scale = scale / (part * scale + part_o * jnp.exp(high_o - top))
        scaled.append((member[o].astype(F32) * scale).astype(BF16))
    members = jnp.concatenate(scaled, axis=1)

    def first_sum_b(h):
        columns = slice(first_z + width * h, first_z + width * (h + 1))
        sums = nn(members, weighted[:, columns])
        for o in range(NY):
            s1b[h, o] = sums[zrows * o : zrows * (o + 1)].astype(BF16)
        for o in ys:
            send(s1b.at[h, o], r1b.at[h, y], p1b_sem.at[h, y], at_y(o))

    width = s1b.shape[3]
    first_sum_b(0)

    swapped = iota((krows, krows), 0)
    swapped = ((swapped // rows) % NY) * zrows + (swapped // yrows) * rows + swapped % rows
    swap = (iota((krows, krows), 1) == swapped).astype(BF16)
    members_z = nn(swap, members).astype(BF16)
    hot_all = jnp.concatenate([hot_t[o] for o in range(NX)], axis=1)
    counts = nt(members_z, hot_all)
    sums = nn(members_z, weighted[:, :first_z])
    for o in range(NZ):
        s1a[o, :, :first_z] = sums[yrows * o : yrows * (o + 1)].astype(BF16)
        s1a[o, :, first_z:] = counts[yrows * o : yrows * (o + 1)].astype(BF16)
    for o in zs:
        send(s1a.at[o], r1a.at[z], p1a_sem.at[z], at_z(o))

    for h in range(1, SUM_STEPS):
        first_sum_b(h)

    by_row = jnp.sum(members.astype(F32), axis=1, keepdims=True)
    mass = jnp.sum(jnp.where(class_hot, by_row, 0.0), axis=0, keepdims=True)
    mass_z[z] = jnp.broadcast_to(mass, mass_z.shape[1:])
    for o in zs:
        send(mass_z.at[z], mass_z.at[z], mz_sem.at[z], at_z(o))

    tb[zrows:, :] = jnp.zeros((tb.shape[0] - zrows, tb.shape[1]), F32)
    ta[yrows:, :] = jnp.zeros((ta.shape[0] - yrows, ta.shape[1]), F32)

    def second_sum_b(h):
        for o in ys:
            arrived(r1b.at[h, o], p1b_sem.at[h, o])
        acc = s1b[h, y].astype(F32)
        for o in ys:
            acc += r1b[h, o].astype(F32)
        tb[:zrows, :] = acc
        for o in range(NZ):
            s2b[h, o] = tb[rows * o : rows * (o + 1), :].astype(BF16)
        for o in zs:
            send(s2b.at[h, o], r2b.at[h, z], p2b_sem.at[h, z], at_z(o))

    def second_sum_a():
        for o in zs:
            arrived(r1a.at[o], p1a_sem.at[o])
        acc = s1a[z].astype(F32)
        for o in zs:
            acc += r1a[o].astype(F32)
        ta[:yrows, :] = acc
        for o in range(NY):
            s2a[o] = ta[rows * o : rows * o + 8, :].astype(BF16)
        for o in ys:
            send(s2a.at[o], r2a.at[y], p2a_sem.at[y], at_y(o))

    second_sum_b(0)
    second_sum_a()
    for h in range(1, SUM_STEPS):
        second_sum_b(h)

    for o in zs:
        arrived(mass_z.at[o], mz_sem.at[o])
    mass = mass_z[0]
    for o in range(1, NZ):
        mass += mass_z[o]
    mass_y[y] = mass
    for o in ys:
        send(mass_y.at[y], mass_y.at[y], my_sem.at[y], at_y(o))

    for o in ys:
        arrived(r2a.at[o], p2a_sem.at[o])
    acc = s2a[y].astype(F32)
    for o in ys:
        acc += r2a[o].astype(F32)
    counted = jnp.concatenate([term.astype(F32) for term in pieces(acc[:, first_z:], 3)], axis=0).astype(BF16)
    filtered = nn(jnp.concatenate([counted, counted], axis=1), square2[...])
    denominator = filtered[0:8] + filtered[8:16] + filtered[16:24] + prior[...]
    out_ref[:, :first_z] = (acc[:, :first_z] / denominator[:, :first_z])[:rows]
    inverse = 1.0 / denominator[:, first_z:]

    for o in ys:
        arrived(mass_y.at[o], my_sem.at[o])
    mass = mass_y[0]
    for o in range(1, NY):
        mass += mass_y[o]
    mass_c[0] = mass
    send(mass_c.at[0], mass_c.at[1], mc_sem, other_core)
    arrived(mass_c.at[1], mc_sem)
    mass = (mass_c[0] + mass_c[1])[0] * (logp.shape[1] / (parts * NZ * NY * NC))
    mass_ref[...] = mass

    for h in range(SUM_STEPS):
        for o in zs:
            arrived(r2b.at[h, o], p2b_sem.at[h, o])
        acc = s2b[h, z].astype(F32)
        for o in zs:
            acc += r2b[h, o].astype(F32)
        columns = slice(width * h, width * (h + 1))
        out_ref[:, first_z + width * h : first_z + width * (h + 1)] = acc * inverse[:rows, columns]

    for copy in sent:
        copy.wait_send()


SENDS = max(SCORE_STEPS, SUM_STEPS) * (5 * (NZ - 1) + 5 * (NY - 1) + 2 * (NX - 1) + 6)


def body(images, ctf_group, projections, ctf_table, noise_power, prior, log_prior, projection_class):
    parts, pixels = images.shape
    groups = ctf_table.shape[0]
    classes = log_prior.shape[0]
    rows = projections.shape[0]
    cut, first_z = GATHER_Z, SUM_Z
    width = (pixels - first_z) // SUM_STEPS
    krows = NZ * NY * rows
    zrows, yrows = NZ * rows, NY * rows
    chip = NC * parts
    block = chip // NX
    pad = 8

    def up(n):
        return -(-n // pad) * pad

    vmem = pltpu.VMEM
    dma = pltpu.SemaphoreType.DMA
    sums, mass = pl.pallas_call(
        kernel,
        out_shape=(
            jax.ShapeDtypeStruct((rows, pixels), F32),
            jax.ShapeDtypeStruct((classes,), F32),
        ),
        in_specs=[pl.BlockSpec(memory_space=pl.ANY)] * 8,
        out_specs=[pl.BlockSpec(memory_space=pltpu.VMEM)] * 2,
        scratch_shapes=[
            vmem((parts, pixels), BF16),
            vmem((groups, pixels), F32),
            vmem((1, pixels), F32),
            vmem((1, pixels), F32),
            vmem((1, classes), F32),
            vmem((NC * krows,), jnp.int32),
            vmem((NC, 1, parts), jnp.int32),
            vmem((rows, cut), BF16),
            vmem((rows, pixels - cut), BF16),
            vmem((NZ, rows, cut), BF16),
            vmem((NY, rows, pixels - cut), BF16),
            vmem((NY, zrows, cut), BF16),
            vmem((NZ, yrows, pixels - cut), BF16),
            vmem((zrows, cut), F32),
            vmem((krows, pixels - cut), F32),
            vmem((3 * groups, pixels), BF16),
            vmem((2 * groups, pixels), BF16),
            vmem((chip, pixels), BF16),
            vmem((NX, groups, block), BF16),
            vmem((SCORE_STEPS, NX, krows // SCORE_STEPS, block), F32),
            vmem((SCORE_STEPS, NX, krows // SCORE_STEPS, block), F32),
            vmem((SCORE_STEPS, 2, krows // SCORE_STEPS, block), F32),
            vmem((NX, NC, 8, block), F32),
            vmem((NX, krows, block), BF16),
            vmem((NZ, yrows, first_z + groups), BF16),
            vmem((SUM_STEPS, NY, zrows, width), BF16),
            vmem((NZ, yrows, first_z + groups), BF16),
            vmem((SUM_STEPS, NY, zrows, width), BF16),
            vmem((up(rows * (NY - 1) + 8), first_z + groups), F32),
            vmem((up(rows * (NZ - 1) + 8), width), F32),
            vmem((NY, 8, first_z + groups), BF16),
            vmem((SUM_STEPS, NZ, rows, width), BF16),
            vmem((NY, 8, first_z + groups), BF16),
            vmem((SUM_STEPS, NZ, rows, width), BF16),
            vmem((2, 8, classes), F32),
            vmem((NZ, 8, classes), F32),
            vmem((NY, 8, classes), F32),
            dma((9,)),
            dma((SENDS,)),
            dma, dma,
            dma((NZ,)), dma((NY,)), dma((NY,)), dma((NZ,)),
            dma((SCORE_STEPS, NX)), dma((SCORE_STEPS,)), dma((NX, NC)), dma((NX,)),
            dma((NZ,)), dma((SUM_STEPS, NY)), dma((NY,)), dma((SUM_STEPS, NZ)),
            dma, dma((NZ,)), dma((NY,)),
        ],
        compiler_params=pltpu.CompilerParams(
            collective_id=0, has_side_effects=True, vmem_limit_bytes=56 * 1024 * 1024
        ),
        cost_estimate=pl.CostEstimate(
            flops=4 * chip * krows * pixels, bytes_accessed=4 * parts * pixels, transcendentals=krows * block
        ),
    )(
        images,
        ctf_group.reshape(1, parts),
        projections,
        ctf_table,
        noise_power.reshape(1, pixels),
        prior.reshape(1, pixels),
        log_prior.reshape(1, classes),
        projection_class,
    )
    return sums, mass


def solution(mesh):
    placed = (
        P("dom", "pix"),
        P("dom"),
        P("dom", "pix"),
        P(None, "pix"),
        P("pix"),
        P("pix"),
        P(),
        P(),
    )
    return jax.shard_map(
        body, mesh=mesh, in_specs=placed, out_specs=(P("dom", "pix"), P()), check_vma=False
    )
```

```python
import functools

import jax
import jax.numpy as jnp
from jax import lax
from jax.experimental import pallas as pl
from jax.experimental.pallas import tpu as pltpu
from jax.sharding import PartitionSpec as P

MESH = pl.DeviceIdType.MESH
F32 = jnp.float32
BF16 = jnp.bfloat16
NZ, NY, NC, NX, NF = 8, 4, 2, 4, 2
GATHER_Z, SUM_Z = 1024, 768
SCORE_STEPS, SUM_STEPS = 2, 2


def nt(a, b):
    return lax.dot_general(a, b, (((1,), (1,)), ((), ())), preferred_element_type=F32)


def nn(a, b):
    return lax.dot_general(a, b, (((1,), (0,)), ((), ())), preferred_element_type=F32)


def pieces(a, count):
    terms = []
    for _ in range(count):
        term = a.astype(BF16)
        terms.append(term)
        a = a - term.astype(F32)
    return terms


def iota(shape, axis):
    return lax.broadcasted_iota(jnp.int32, shape, axis)


def kernel(
    images_hbm, group_hbm, proj_hbm, ctf_hbm, noise_hbm, prior_hbm, logp_hbm, class_hbm,
    out_ref, mass_ref,
    images, ctf, noise, prior, logp, pclass, group, own_a, own_b,
    ra1, rb1, ra2, rb2, compact_a, compact_b, table3, square2, weighted, hot_t,
    scores, rx, ry, stats, member, s1a, s1b, r1a, r1b, ta, tb, s2a, s2b, r2a, r2b,
    mass_c, mass_z, mass_y,
    load_sem, send_sem, group_sem, w_sem, a1_sem, b1_sem, a2_sem, b2_sem, x_sem, y_sem, st_sem, m_sem,
    p1a_sem, p1b_sem, p2a_sem, p2b_sem, mc_sem, mz_sem, my_sem,
):
    dom, pix = lax.axis_index("dom"), lax.axis_index("pix")
    core, z, y = dom % NC, (dom // NC) % NZ, dom // (NC * NZ)
    x, far = pix // NF, pix % NF
    rows, cut = own_a.shape
    parts = images.shape[0]
    groups, pixels = ctf.shape
    first_z = s1a.shape[2] - groups
    zrows = NZ * rows
    yrows = NY * rows
    krows = NY * NZ * rows
    block = NC * parts // NX

    def at_z(o):
        return ((y * NZ + o) * NC + core, pix)

    def at_y(o):
        return ((o * NZ + z) * NC + core, pix)

    def at_x(o):
        return (dom, o * NF + far)

    other_core = ((y * NZ + z) * NC + (1 - core), pix)
    other_far = (dom, x * NF + (1 - far))
    zs = [(z + d) % NZ for d in (4, 3, 5, 2, 6, 1, 7)[8 - NZ :]]
    ys = [(y + d) % NY for d in (2, 1, 3)[4 - NY :]]
    xs = [(x + d) % NX for d in (2, 1, 3)[4 - NX :]]

    sent = []

    def send(src, dst, recv_sem, device):
        copy = pltpu.make_async_remote_copy(
            src_ref=src,
            dst_ref=dst,
            send_sem=send_sem.at[len(sent)],
            recv_sem=recv_sem,
            device_id=device,
            device_id_type=MESH,
        )
        copy.start()
        sent.append(copy)

    def arrived(dst, recv_sem):
        pltpu.make_async_remote_copy(
            src_ref=dst,
            dst_ref=dst,
            send_sem=recv_sem,
            recv_sem=recv_sem,
            device_id=other_core,
            device_id_type=MESH,
        ).wait_recv()

    loads = [
        pltpu.make_async_copy(src, dst, load_sem.at[i])
        for i, (src, dst) in enumerate((
            (proj_hbm.at[:, pl.ds(0, cut)], own_a),
            (proj_hbm.at[:, pl.ds(cut, pixels - cut)], own_b),
            (group_hbm, group.at[core]),
            (ctf_hbm, ctf),
            (noise_hbm, noise),
            (images_hbm, images),
            (prior_hbm, prior),
            (logp_hbm, logp),
            (class_hbm, pclass),
        ))
    ]
    for copy in loads:
        copy.start()

    barrier = pltpu.get_barrier_semaphore()
    peers = [at_z(o) for o in zs] + [at_y(o) for o in ys] + [at_x(o) for o in xs]
    peers += [other_core, other_far]
    for peer in peers:
        pl.semaphore_signal(barrier, inc=1, device_id=peer, device_id_type=MESH)
    for copy in loads[:3]:
        copy.wait()
    pl.semaphore_wait(barrier, len(peers))

    for o in zs:
        send(own_a, ra1.at[z], a1_sem.at[z], at_z(o))
    for o in ys:
        send(own_b, rb1.at[y], b1_sem.at[y], at_y(o))
    send(group.at[core], group.at[core], group_sem, other_core)
    ra1[z] = own_a[...]
    rb1[y] = own_b[...]

    for copy in loads[3:]:
        copy.wait()

    def second_a():
        for o in zs:
            arrived(ra1.at[o], a1_sem.at[o])
        for o in range(NZ):
            compact_a[rows * o : rows * (o + 1), :] = ra1[o].astype(F32)
        ra2[y] = compact_a[...].astype(BF16)
        for o in ys:
            send(ra2.at[y], ra2.at[y], a2_sem.at[y], at_y(o))

    def second_b():
        for o in ys:
            arrived(rb1.at[o], b1_sem.at[o])
        for o in range(NY):
            compact_b[rows * o : rows * (o + 1), :] = rb1[o].astype(F32)
        rb2[z] = compact_b[:yrows, :].astype(BF16)
        for o in zs:
            send(rb2.at[z], rb2.at[z], b2_sem.at[z], at_z(o))

    second_b()
    second_a()

    chunk = min(512, pixels)
    own_hot = jnp.transpose((iota((groups, parts), 0) == group[core]).astype(F32)).astype(BF16)
    hot3 = jnp.concatenate([own_hot] * 3, axis=1)
    mine = pl.ds(pl.multiple_of(core * parts, parts), parts)
    for c in range(0, pixels, chunk):
        columns = slice(c, c + chunk)
        table, variance = ctf[:, columns], noise[:, columns]
        for i, term in enumerate(pieces(table / variance, 3)):
            table3[groups * i : groups * (i + 1), columns] = term
        for i, term in enumerate(pieces(table * table / variance, 2)):
            square2[groups * i : groups * (i + 1), columns] = term
        weights = nn(hot3, table3[:, columns])
        weighted[mine, columns] = (images[:, columns].astype(F32) * weights).astype(BF16)
    send(weighted.at[mine], weighted.at[mine], w_sem, other_core)
    theirs = pl.ds(pl.multiple_of((1 - core) * parts, parts), parts)

    owner = ((iota((krows, 1), 0) // rows) * NC + core) * rows + iota((krows, 1), 0) % rows
    picked = iota((krows, NC * krows), 1) == owner
    row_class = jnp.sum(jnp.where(picked, pclass[...].reshape(1, NC * krows), 0), axis=1, keepdims=True)
    class_hot = row_class == iota((krows, logp.shape[1]), 1)
    bias = jnp.sum(jnp.where(class_hot, logp[...], 0.0), axis=1, keepdims=True)

    arrived(group.at[1 - core], group_sem)
    for o in range(NX):
        first = o * block % parts
        hot_t[o] = (iota((groups, block), 0) == group[o * block // parts, :, first : first + block]).astype(BF16)

    arrived(weighted.at[theirs], w_sem)

    def squares(proj, columns):
        wide = proj.astype(F32)
        high, low = pieces(wide * wide, 2)
        return nt(high, square2[:, columns]) + nt(low, square2[:, columns])

    for o in ys:
        arrived(ra2.at[o], a2_sem.at[o])
    proj_a = ra2[...].reshape(krows, cut)
    cross = nt(proj_a, weighted[:, :cut])
    for h in range(SCORE_STEPS):
        some = slice(krows // SCORE_STEPS * h, krows // SCORE_STEPS * (h + 1))
        for o in range(NX):
            scores[h, o] = cross[some, block * o : block * (o + 1)]
    norm_a = squares(proj_a, slice(0, cut))

    for o in zs:
        arrived(rb2.at[o], b2_sem.at[o])
    for o in range(NZ):
        wide = rb2[o].astype(F32)
        for p in range(NY):
            first = p * zrows + o * rows
            compact_b[first : first + rows, :] = wide[rows * p : rows * (p + 1)]
    proj_b = compact_b[...].astype(BF16)
    norm2 = norm_a + squares(proj_b, slice(cut, pixels))
    norm = norm2[:, :groups] + norm2[:, groups:]
    norm3 = jnp.concatenate([term for term in pieces(-0.5 * norm, 3)], axis=1)
    part = krows // SCORE_STEPS
    for h in range(SCORE_STEPS):
        some = slice(part * h, part * (h + 1))
        for o in [*xs, x]:
            these = pl.ds(pl.multiple_of(o * block, block), block)
            hot3 = jnp.concatenate([hot_t[o]] * 3, axis=0)
            scores[h, o] += nt(proj_b[some], weighted[these, cut:]) + nn(norm3[some], hot3)
            if o is not x:
                send(scores.at[h, o], rx.at[h, x], x_sem.at[h, x], at_x(o))
    for h in range(SCORE_STEPS):
        for o in xs:
            arrived(rx.at[h, o], x_sem.at[h, o])
        score = scores[h, x]
        for o in xs:
            score += rx[h, o]
        ry[h, 0] = score
        send(ry.at[h, 0], ry.at[h, 1], y_sem.at[h], other_far)
    for h in range(SCORE_STEPS):
        arrived(ry.at[h, 1], y_sem.at[h])
    score = jnp.concatenate([ry[h, 0] + ry[h, 1] for h in range(SCORE_STEPS)], axis=0) + bias

    high = jnp.max(score, axis=0, keepdims=True)
    raised = jnp.exp(score - high)
    part = jnp.sum(raised, axis=0, keepdims=True)
    stats[0, 0:1] = high
    stats[0, 1:2] = part
    send(stats.at[0], stats.at[1], st_sem, other_core)
    arrived(stats.at[1], st_sem)
    high_o, part_o = stats[1, 0:1], stats[1, 1:2]
    top = jnp.maximum(high, high_o)
    scale = jnp.exp(high - top)
    scale = scale / (part * scale + part_o * jnp.exp(high_o - top))
    member[x] = (raised * scale).astype(BF16)
    for o in xs:
        send(member.at[x], member.at[x], m_sem.at[x], at_x(o))
    for o in xs:
        arrived(member.at[o], m_sem.at[o])
    members = jnp.concatenate([member[o] for o in range(NX)], axis=1)

    def first_sum_b(h):
        columns = slice(first_z + width * h, first_z + width * (h + 1))
        sums = nn(members, weighted[:, columns])
        for o in range(NY):
            s1b[h, o] = sums[zrows * o : zrows * (o + 1)].astype(BF16)
        for o in ys:
            send(s1b.at[h, o], r1b.at[h, y], p1b_sem.at[h, y], at_y(o))

    width = s1b.shape[3]
    first_sum_b(0)

    swapped = iota((krows, krows), 0)
    swapped = ((swapped // rows) % NY) * zrows + (swapped // yrows) * rows + swapped % rows
    swap = (iota((krows, krows), 1) == swapped).astype(BF16)
    members_z = nn(swap, members).astype(BF16)
    hot_all = jnp.concatenate([hot_t[o] for o in range(NX)], axis=1)
    counts = nt(members_z, hot_all)
    sums = nn(members_z, weighted[:, :first_z])
    for o in range(NZ):
        s1a[o, :, :first_z] = sums[yrows * o : yrows * (o + 1)].astype(BF16)
        s1a[o, :, first_z:] = counts[yrows * o : yrows * (o + 1)].astype(BF16)
    for o in zs:
        send(s1a.at[o], r1a.at[z], p1a_sem.at[z], at_z(o))

    for h in range(1, SUM_STEPS):
        first_sum_b(h)

    by_row = jnp.sum(members.astype(F32), axis=1, keepdims=True)
    mass = jnp.sum(jnp.where(class_hot, by_row, 0.0), axis=0, keepdims=True)
    mass_z[z] = jnp.broadcast_to(mass, mass_z.shape[1:])
    for o in zs:
        send(mass_z.at[z], mass_z.at[z], mz_sem.at[z], at_z(o))

    tb[zrows:, :] = jnp.zeros((tb.shape[0] - zrows, tb.shape[1]), F32)
    ta[yrows:, :] = jnp.zeros((ta.shape[0] - yrows, ta.shape[1]), F32)

    def second_sum_b(h):
        for o in ys:
            arrived(r1b.at[h, o], p1b_sem.at[h, o])
        acc = s1b[h, y].astype(F32)
        for o in ys:
            acc += r1b[h, o].astype(F32)
        tb[:zrows, :] = acc
        for o in range(NZ):
            s2b[h, o] = tb[rows * o : rows * (o + 1), :].astype(BF16)
        for o in zs:
            send(s2b.at[h, o], r2b.at[h, z], p2b_sem.at[h, z], at_z(o))

    def second_sum_a():
        for o in zs:
            arrived(r1a.at[o], p1a_sem.at[o])
        acc = s1a[z].astype(F32)
        for o in zs:
            acc += r1a[o].astype(F32)
        ta[:yrows, :] = acc
        for o in range(NY):
            s2a[o] = ta[rows * o : rows * o + 8, :].astype(BF16)
        for o in ys:
            send(s2a.at[o], r2a.at[y], p2a_sem.at[y], at_y(o))

    second_sum_b(0)
    second_sum_a()

    for o in zs:
        arrived(mass_z.at[o], mz_sem.at[o])
    mass = mass_z[0]
    for o in range(1, NZ):
        mass += mass_z[o]
    mass_y[y] = mass
    for o in ys:
        send(mass_y.at[y], mass_y.at[y], my_sem.at[y], at_y(o))

    for h in range(1, SUM_STEPS):
        second_sum_b(h)

    for o in ys:
        arrived(r2a.at[o], p2a_sem.at[o])
    acc = s2a[y].astype(F32)
    for o in ys:
        acc += r2a[o].astype(F32)
    counted = jnp.concatenate([term.astype(F32) for term in pieces(acc[:, first_z:], 3)], axis=0).astype(BF16)
    filtered = nn(jnp.concatenate([counted, counted], axis=1), square2[...])
    denominator = filtered[0:8] + filtered[8:16] + filtered[16:24] + prior[...]
    out_ref[:, :first_z] = (acc[:, :first_z] / denominator[:, :first_z])[:rows]
    inverse = 1.0 / denominator[:, first_z:]

    for o in ys:
        arrived(mass_y.at[o], my_sem.at[o])
    mass = mass_y[0]
    for o in range(1, NY):
        mass += mass_y[o]
    mass_c[0] = mass
    send(mass_c.at[0], mass_c.at[1], mc_sem, other_core)
    arrived(mass_c.at[1], mc_sem)
    mass = (mass_c[0] + mass_c[1])[0] * (logp.shape[1] / (parts * NZ * NY * NC))
    mass_ref[...] = mass

    for h in range(SUM_STEPS):
        for o in zs:
            arrived(r2b.at[h, o], p2b_sem.at[h, o])
        acc = s2b[h, z].astype(F32)
        for o in zs:
            acc += r2b[h, o].astype(F32)
        columns = slice(width * h, width * (h + 1))
        out_ref[:, first_z + width * h : first_z + width * (h + 1)] = acc * inverse[:rows, columns]

    for copy in sent:
        copy.wait_send()


SENDS = max(SCORE_STEPS, SUM_STEPS) * (5 * (NZ - 1) + 5 * (NY - 1) + 2 * (NX - 1) + 6)


def body(images, ctf_group, projections, ctf_table, noise_power, prior, log_prior, projection_class):
    parts, pixels = images.shape
    groups = ctf_table.shape[0]
    classes = log_prior.shape[0]
    rows = projections.shape[0]
    cut, first_z = GATHER_Z, SUM_Z
    width = (pixels - first_z) // SUM_STEPS
    krows = NZ * NY * rows
    zrows, yrows = NZ * rows, NY * rows
    chip = NC * parts
    block = chip // NX
    pad = 8

    def up(n):
        return -(-n // pad) * pad

    vmem = pltpu.VMEM
    dma = pltpu.SemaphoreType.DMA
    sums, mass = pl.pallas_call(
        kernel,
        out_shape=(
            jax.ShapeDtypeStruct((rows, pixels), F32),
            jax.ShapeDtypeStruct((classes,), F32),
        ),
        in_specs=[pl.BlockSpec(memory_space=pl.ANY)] * 8,
        out_specs=[pl.BlockSpec(memory_space=pltpu.VMEM)] * 2,
        scratch_shapes=[
            vmem((parts, pixels), BF16),
            vmem((groups, pixels), F32),
            vmem((1, pixels), F32),
            vmem((1, pixels), F32),
            vmem((1, classes), F32),
            vmem((NC * krows,), jnp.int32),
            vmem((NC, 1, parts), jnp.int32),
            vmem((rows, cut), BF16),
            vmem((rows, pixels - cut), BF16),
            vmem((NZ, rows, cut), BF16),
            vmem((NY, rows, pixels - cut), BF16),
            vmem((NY, zrows, cut), BF16),
            vmem((NZ, yrows, pixels - cut), BF16),
            vmem((zrows, cut), F32),
            vmem((krows, pixels - cut), F32),
            vmem((3 * groups, pixels), BF16),
            vmem((2 * groups, pixels), BF16),
            vmem((chip, pixels), BF16),
            vmem((NX, groups, block), BF16),
            vmem((SCORE_STEPS, NX, krows // SCORE_STEPS, block), F32),
            vmem((SCORE_STEPS, NX, krows // SCORE_STEPS, block), F32),
            vmem((SCORE_STEPS, 2, krows // SCORE_STEPS, block), F32),
            vmem((2, 8, block), F32),
            vmem((NX, krows, block), BF16),
            vmem((NZ, yrows, first_z + groups), BF16),
            vmem((SUM_STEPS, NY, zrows, width), BF16),
            vmem((NZ, yrows, first_z + groups), BF16),
            vmem((SUM_STEPS, NY, zrows, width), BF16),
            vmem((up(rows * (NY - 1) + 8), first_z + groups), F32),
            vmem((up(rows * (NZ - 1) + 8), width), F32),
            vmem((NY, 8, first_z + groups), BF16),
            vmem((SUM_STEPS, NZ, rows, width), BF16),
            vmem((NY, 8, first_z + groups), BF16),
            vmem((SUM_STEPS, NZ, rows, width), BF16),
            vmem((2, 8, classes), F32),
            vmem((NZ, 8, classes), F32),
            vmem((NY, 8, classes), F32),
            dma((9,)),
            dma((SENDS,)),
            dma, dma,
            dma((NZ,)), dma((NY,)), dma((NY,)), dma((NZ,)),
            dma((SCORE_STEPS, NX)), dma((SCORE_STEPS,)), dma, dma((NX,)),
            dma((NZ,)), dma((SUM_STEPS, NY)), dma((NY,)), dma((SUM_STEPS, NZ)),
            dma, dma((NZ,)), dma((NY,)),
        ],
        compiler_params=pltpu.CompilerParams(
            collective_id=0, has_side_effects=True, vmem_limit_bytes=56 * 1024 * 1024
        ),
        cost_estimate=pl.CostEstimate(
            flops=4 * chip * krows * pixels, bytes_accessed=4 * parts * pixels, transcendentals=krows * block
        ),
    )(
        images,
        ctf_group.reshape(1, parts),
        projections,
        ctf_table,
        noise_power.reshape(1, pixels),
        prior.reshape(1, pixels),
        log_prior.reshape(1, classes),
        projection_class,
    )
    return sums, mass


def solution(mesh):
    placed = (
        P("dom", "pix"),
        P("dom"),
        P("dom", "pix"),
        P(None, "pix"),
        P("pix"),
        P("pix"),
        P(),
        P(),
    )
    return jax.shard_map(
        body, mesh=mesh, in_specs=placed, out_specs=(P("dom", "pix"), P()), check_vma=False
    )
```
